32 devices in a mesh: dp: 4 (over z), fsdp: 8 (over y, x, core).
Axes of the slice: x: 2, y: 2, z: 4, core: 2. Of those that a mesh axis runs over, the one named last changes fastest.
Arguments:
- item_hidden: bfloat16 [2048, 2048], P(('dp', 'fsdp')), may hold values from -400 to 400
- item_gain: float32 [2048], replicated, may hold values from 0.25 to 1.75
- history: int32 [4096], P(('dp', 'fsdp')), may hold values from 0 to 255, as said below
- owner_map: int32 [8, 256], P('fsdp'), may hold values from 0 to 255, as said below
- user_gain: float32 [2048], replicated, may hold values from 0.25 to 1.75
- value_weight: bfloat16 [2048, 2048], P('fsdp'), may hold values from -0.125 to 0.125
- value_grad: bfloat16 [4096, 2048], P(('dp', 'fsdp')), may hold values from -6 to 6
Outputs:
- values: bfloat16 [4096, 2048], P(('dp', 'fsdp'))
- item_grad: float32 [2048, 2048], P(('dp', 'fsdp'))
The draws below stay inside these ranges and needn't reach their ends.
Inputs may be any that keep to these rules, and one draw needn't show every extreme that they name: `history`: storage row s of catalog c is row s % 64 of the items on dp index s // 64 and fsdp index c. In each aligned block of 128 positions, the positions name at most 8 distinct items stored on any one dp index, and exactly 8 for some dp index. `owner_map`: each row is a permutation.
All inputs are finite; a program needn't handle non-finite values.
Results may differ from the reference program's by a relative error of at most 0.0057.
Values may be sent and summed in bfloat16 or wider, within the bound.
A program may use at most 64 MiB of HBM per device.

```python
import math
import jax
import jax.numpy as jnp
from jax import lax

D = 2048
CAP = 8
ITEM_DEV = 64
HIST_DEV = 128
KVW = 2048
ITEMS = 2048
POSITIONS = 4096
N_DP = 4
N_FSDP = 8


def owner_table(key):
    keys = jax.random.split(jax.random.fold_in(key, 11), N_FSDP)
    return jax.vmap(lambda single: jax.random.permutation(single, ITEM_DEV * N_DP))(keys).astype(jnp.int32)


def draw_owner_map(key, part):
    table = owner_table(key)
    return table


def draw_history(key, part):
    table = owner_table(key)
    key = jax.random.fold_in(key, 5)
    blocks = N_DP * N_FSDP
    first_key, second_key, third_key, fourth_key, fifth_key = jax.random.split(key, 5)
    counts = jax.random.randint(first_key, (blocks, N_DP), max(CAP // 2, 1), CAP + 1)
    fullest = jax.random.randint(second_key, (blocks,), 0, N_DP)
    counts = jnp.where(jnp.arange(N_DP)[None, :] == fullest[:, None], CAP, counts)
    perm_keys = jax.random.split(third_key, blocks * N_DP)
    ranks = jax.vmap(lambda single: jax.random.permutation(single, ITEM_DEV))(perm_keys).reshape(blocks, N_DP, ITEM_DEV)
    chosen = (ranks < counts[:, :, None]).reshape(blocks, N_DP * ITEM_DEV)
    order = jnp.argsort(jnp.where(chosen, 0, 1), axis=1, stable=True).astype(jnp.int32)
    total = jnp.sum(counts, axis=1)
    place = jnp.arange(HIST_DEV)[None, :]
    one_pick = jax.random.randint(fourth_key, (blocks, HIST_DEV), 0, 1 << 20) % total[:, None]
    two_pick = jax.random.randint(fifth_key, (blocks, HIST_DEV), 0, 1 << 20) % total[:, None]
    pick = jnp.where(place < total[:, None], place, jnp.minimum(one_pick, two_pick))
    stored = jnp.take_along_axis(order, pick, axis=1)
    column = jnp.arange(blocks) % N_FSDP
    inverse = jnp.argsort(table, axis=1, stable=True).astype(jnp.int32)
    items = jnp.take_along_axis(inverse[column], stored, axis=1)
    return items.reshape(-1).astype(jnp.int32)


def draw_item_hidden(key, part):
    key = jax.random.fold_in(key, 7)
    row_key, col_key, base_key = jax.random.split(key, 3)
    rows = jnp.exp(jax.random.uniform(row_key, (ITEMS, 1), jnp.float32, 0.0, math.log(10.0)))
    cols = jnp.exp(jax.random.uniform(col_key, (1, D), jnp.float32, 0.0, math.log(10.0)))
    base = jnp.clip(jax.random.normal(base_key, (ITEMS, D), jnp.float32), -4.0, 4.0)
    return (base * rows * cols).astype(jnp.bfloat16)


def steps_of(stream_key, dims, pieces, smallest, largest):
    factor_of = 1.0
    for axis_at, parts in pieces:
        heights = jax.random.uniform(jax.random.fold_in(jax.random.fold_in(stream_key, 6), axis_at), (parts,), jnp.float32, smallest / len(pieces), largest / len(pieces))
        factor_of = factor_of * jnp.repeat(jnp.exp(heights), dims[axis_at] // parts).reshape((-1,) + (1,) * (len(dims) - 1 - axis_at))
    return factor_of


def scatter_about(key, dims, spread, limit, cuts=(), kind=jnp.bfloat16):
    result = spread * jax.random.normal(key, dims, jnp.float32)
    if cuts:
        result = result * steps_of(key, dims, cuts, -0.22, 0.18)
    return jnp.clip(result, -limit, limit).astype(kind)


def setup_inputs(seed: int = 0) -> dict:
    streams_of = jax.random.split(jax.random.key(seed), 8)
    return {
        "item_hidden": draw_item_hidden(jax.random.fold_in(streams_of[7], 71), 0),
        "item_gain": jnp.clip(1.0 + 0.15 * jax.random.normal(streams_of[1], (D,), jnp.float32), 0.25, 1.75),
        "history": draw_history(jax.random.fold_in(streams_of[7], 71), 0),
        "owner_map": draw_owner_map(jax.random.fold_in(streams_of[7], 71), 0),
        "user_gain": jnp.clip(1.0 + 0.15 * jax.random.normal(streams_of[4], (D,), jnp.float32), 0.25, 1.75),
        "value_weight": scatter_about(streams_of[5], (D, KVW), D ** -0.5, 0.125, ((0, 8),)),
        "value_grad": scatter_about(streams_of[6], (POSITIONS, KVW), 1.0, 6.0, ((0, 32),)),
    }


eps = 1e-06

def norm_rows(values, gain):
    scale = lax.rsqrt(lax.optimization_barrier(jnp.mean(values * values, axis=1, keepdims=True)) + eps)
    return (values * scale * gain, scale)

def norm_back(values, gain, scale, upstream):
    unit = values * scale
    scaled = upstream * gain
    return scale * (scaled - unit * lax.optimization_barrier(jnp.mean(scaled * unit, axis=1, keepdims=True)))

def reference(item_hidden, item_gain, history, owner_map, user_gain, value_weight, value_grad):
    hidden = item_hidden.astype(jnp.float32)
    item_emb, item_scale = norm_rows(hidden, item_gain)
    item_emb = item_emb.astype(jnp.bfloat16)
    blocks = N_DP * N_FSDP
    hist = history.reshape(blocks, HIST_DEV)
    grads = value_grad.reshape(blocks, HIST_DEV, KVW)
    lower = jnp.arange(HIST_DEV, dtype=jnp.int32)[:, None] > jnp.arange(HIST_DEV, dtype=jnp.int32)[None, :]

    def one_block(total, inputs):
        ids, upstream_rows, block = inputs
        column = block % N_FSDP
        stored = jnp.take(owner_map[column], ids).astype(jnp.int32)
        rows = (stored // ITEM_DEV * N_FSDP + column) * ITEM_DEV + stored % ITEM_DEV
        x = jnp.take(item_emb, rows, axis=0).astype(jnp.float32)
        normed, scale = norm_rows(x, user_gain)
        normed = normed.astype(jnp.bfloat16)
        values = jnp.dot(normed, value_weight, preferred_element_type=jnp.float32).astype(jnp.bfloat16)
        upstream = jnp.dot(upstream_rows, value_weight.T, preferred_element_type=jnp.float32)
        dx = norm_back(x, user_gain, scale, upstream)
        same = rows[:, None] == rows[None, :]
        sums = jnp.dot(same.astype(jnp.float32), dx, precision=lax.Precision.HIGHEST, preferred_element_type=jnp.float32)
        sums = lax.optimization_barrier(sums.astype(jnp.bfloat16)).astype(jnp.float32)
        first = jnp.logical_not(jnp.any(same & lower, axis=1))
        contrib = jnp.where(first[:, None], sums, 0.0)
        total = total.at[rows].add(contrib)
        return (total, values)
    total, values = lax.scan(one_block, jnp.zeros((ITEMS, D), jnp.float32), (hist, grads, jnp.arange(blocks, dtype=jnp.int32)))
    item_grad = norm_back(hidden, item_gain, item_scale, total)
    return (values.reshape(POSITIONS, KVW), item_grad)
```

```python
import functools
import jax
import jax.numpy as jnp
from jax import lax
from jax.experimental import pallas as pl
from jax.experimental.pallas import tpu as pltpu
from jax.sharding import PartitionSpec as P

CAP = 8
MESH = pl.DeviceIdType.MESH
f32 = jnp.float32
bf16 = jnp.bfloat16


eps = 1e-06


def norm_rows(values, gain):
    scale = lax.rsqrt(jnp.mean(values * values, axis=1, keepdims=True) + eps)
    return (values * scale * gain, scale)


def norm_back(values, gain, scale, upstream):
    unit = values * scale
    scaled = upstream * gain
    return scale * (scaled - unit * jnp.mean(scaled * unit, axis=1, keepdims=True))


def locate(owner_row, items):
    matches = items[:, None] == lax.broadcasted_iota(
        jnp.int32, (items.shape[0], owner_row.shape[0]), 1
    )
    return jnp.sum(jnp.where(matches, owner_row[None, :], 0), axis=1)


def local_moving_weight(item_hidden, item_gain, history, owner_map, user_gain, value_weight, value_grad):
    groups = lax.axis_size("dp")
    here = lax.axis_index("dp")
    item_rows = item_hidden.shape[0]
    hist_rows = history.shape[0]
    width = item_hidden.shape[1]
    owner_row = owner_map[0]
    pool = owner_row.shape[0]
    hidden = item_hidden.astype(jnp.float32)
    item_emb, item_scale = norm_rows(hidden, item_gain)
    item_emb = item_emb.astype(jnp.bfloat16)
    all_history = lax.all_gather(history, "dp", axis=0, tiled=True)
    stored_all = locate(owner_row, all_history).reshape(groups, hist_rows)
    local_rows = lax.broadcasted_iota(jnp.int32, (groups, hist_rows, item_rows), 2)
    wanted = jnp.any(stored_all[:, :, None] == here * item_rows + local_rows, axis=1)
    slot = jnp.cumsum(wanted.astype(jnp.int32), axis=1) - 1
    slot_ids = lax.broadcasted_iota(jnp.int32, (groups, CAP, item_rows), 1)
    select = (wanted[:, None, :] & (slot[:, None, :] == slot_ids)).astype(jnp.bfloat16)
    outgoing = jnp.einsum(
        "dcr,rk->dck", select, item_emb, preferred_element_type=jnp.float32
    ).astype(jnp.bfloat16)
    incoming = lax.all_to_all(outgoing, "dp", split_axis=0, concat_axis=0, tiled=True)
    stored = locate(owner_row, history)
    pick = stored[:, None] == lax.broadcasted_iota(jnp.int32, (hist_rows, pool), 1)
    own_wanted = jnp.any(pick, axis=0).reshape(groups, item_rows)
    own_slot = (jnp.cumsum(own_wanted.astype(jnp.int32), axis=1) - 1).reshape(pool)
    slot_pos = jnp.sum(jnp.where(pick, own_slot[None, :], 0), axis=1)
    buffer_row = stored // item_rows * CAP + slot_pos
    x = jnp.take(incoming.reshape(groups * CAP, width), buffer_row, axis=0).astype(jnp.float32)
    normed, scale = norm_rows(x, user_gain)
    normed = normed.astype(jnp.bfloat16)
    whole = lax.all_gather(value_weight, "fsdp", axis=0, tiled=True)
    values = jnp.dot(normed, whole, preferred_element_type=jnp.float32)
    upstream = lax.dot_general(
        value_grad, whole, (((1,), (1,)), ((), ())), preferred_element_type=jnp.float32
    )
    values = values.astype(jnp.bfloat16)
    dx = norm_back(x, user_gain, scale, upstream)
    one_hot = (
        buffer_row[:, None] == lax.broadcasted_iota(jnp.int32, (hist_rows, groups * CAP), 1)
    ).astype(jnp.float32)
    summed = lax.dot_general(
        one_hot,
        dx,
        (((0,), (0,)), ((), ())),
        precision=lax.Precision.HIGHEST,
        preferred_element_type=jnp.float32,
    )
    returned = lax.all_to_all(
        summed.astype(jnp.bfloat16).reshape(groups, CAP, width),
        "dp",
        split_axis=0,
        concat_axis=0,
        tiled=True,
    )
    emb_grad = jnp.einsum("dcr,dck->rk", select, returned, preferred_element_type=jnp.float32)
    item_grad = norm_back(hidden, item_gain, item_scale, emb_grad)
    return (values, item_grad)


def iota(shape, dim):
    return lax.broadcasted_iota(jnp.int32, shape, dim)


def dot(a, b, ca=1, cb=0):
    return lax.dot_general(a, b, (((ca,), (cb,)), ((), ())), preferred_element_type=f32)


def fold(rows):
    half = rows.shape[1] // 2
    return jnp.concatenate([rows[:, :half], rows[:, half:]], axis=0)


def unfold(rows):
    return jnp.concatenate([rows[:CAP], rows[CAP:]], axis=1)


def stored_rows(hist, parts, item_rows):
    pool = parts.shape[1]
    named = (iota((pool, hist.shape[1]), 0) == hist).astype(f32).astype(bf16)
    found = dot(parts, named)
    return found[0:1] * item_rows + found[1:2]


def slots(wants, item_rows):
    lane = iota((item_rows, 128), 1)
    wanted = jnp.zeros((item_rows, 128), f32)
    for group, want in enumerate(wants):
        wanted = jnp.where(lane // CAP == group, want, wanted)
    before = (iota((item_rows, item_rows), 1) < iota((item_rows, item_rows), 0)).astype(f32)
    slot = dot(before.astype(bf16), wanted.astype(bf16))
    return jnp.where(slot == (lane % CAP).astype(f32), wanted, 0.0)


def kernel(
    groups, chips,
    item_gain, history, owner, user_gain, item_hidden, weight, value_grad,
    values_out, item_grad_out,
    hidden_buf, grad_buf, w_buf, hist_buf, emb_out, emb_in, sum_buf, x_out, x_in,
    part_own, part_out, part_in, up_out, up_in, back_out, back_in,
    local_sem, w_sem, hist_send, hist_recv, emb_send, emb_recv, sum_send, sum_recv,
    x_send, x_recv, part_send, part_recv, up_send, up_recv, back_send, back_recv,
):
    here = lax.axis_index("dp")
    fsdp = lax.axis_index("fsdp")
    chip = fsdp // 2
    core = fsdp % 2
    item_rows, width = item_hidden.shape
    hist_rows = history.shape[1]
    rows = groups * CAP
    piece = width // chips
    peers = [lax.rem(here + k, groups) for k in range(1, groups)]
    mates = [lax.rem(chip + k, chips) for k in range(1, chips)]

    def dp_id(peer):
        return (peer, fsdp)

    def chip_id(mate):
        return (here, mate * 2 + core)

    sibling = (here, chip * 2 + 1 - core)

    loads = [
        pltpu.make_async_copy(value_grad, grad_buf, local_sem.at[0]),
        pltpu.make_async_copy(item_hidden, hidden_buf, local_sem.at[1]),
        pltpu.make_async_copy(weight, w_buf.at[core], local_sem.at[2]),
    ]
    for load in loads:
        load.start()

    barrier = pltpu.get_barrier_semaphore()
    for target in [dp_id(p) for p in peers] + [chip_id(m) for m in mates] + [sibling]:
        pl.semaphore_signal(barrier, inc=1, device_id=target, device_id_type=MESH)
    pl.semaphore_wait(barrier, groups + chips - 1)

    def remote(src, dst, send, recv, target):
        return pltpu.make_async_remote_copy(
            src_ref=src, dst_ref=dst, send_sem=send, recv_sem=recv,
            device_id=target, device_id_type=MESH,
        )

    sends = []

    def send_dp(out_of, into, send, recv):
        for k, peer in enumerate(peers):
            copy = remote(out_of(peer), into.at[here], send.at[k], recv.at[here], dp_id(peer))
            copy.start()
            sends.append(copy)

    def wait_dp(into, send, recv):
        for k, peer in enumerate(peers):
            remote(into.at[peer], into.at[peer], send.at[k], recv.at[peer], dp_id(peer)).wait_recv()

    def send_chip(out_of, into, send, recv):
        for k, mate in enumerate(mates):
            copy = remote(out_of(mate), into.at[chip], send.at[k], recv.at[chip], chip_id(mate))
            copy.start()
            sends.append(copy)

    def wait_chip(into, send, recv):
        for k, mate in enumerate(mates):
            remote(into.at[mate], into.at[mate], send.at[k], recv.at[mate], chip_id(mate)).wait_recv()

    send_dp(lambda peer: history, hist_buf, hist_send, hist_recv)
    hist_buf[here] = history[...]

    owner_row = owner[...]
    pool = owner_row.shape[1]
    div = (owner_row // item_rows).astype(f32)
    mod = (owner_row % item_rows).astype(f32)
    parts = jnp.where(iota((8, pool), 0) == 0, div, mod).astype(bf16)

    own = stored_rows(history[...], parts, item_rows)
    match = (iota((pool, hist_rows), 0).astype(f32) == own).astype(f32)
    wants = [
        jnp.max(match[e * item_rows : (e + 1) * item_rows], axis=1, keepdims=True)
        for e in range(groups)
    ]
    one_hot = slots(wants, item_rows)
    lane = iota((item_rows, 128), 1)
    stacked = jnp.concatenate(
        [jnp.where(lane // CAP == e, one_hot, 0.0) for e in range(groups)], axis=0
    )
    place = dot(stacked.astype(bf16), match.astype(bf16), 0, 0)[:rows]
    place = place.astype(bf16)

    loads[0].wait()
    sum_buf[chip] = dot(place, grad_buf[...]).astype(bf16)
    send_chip(lambda mate: sum_buf.at[chip], sum_buf, sum_send, sum_recv)

    w_copy = remote(weight, w_buf.at[core], w_sem.at[0], w_sem.at[1], sibling)
    w_copy.start()

    loads[1].wait()
    hidden = hidden_buf[...].astype(f32)
    item_scale = lax.rsqrt(jnp.mean(hidden * hidden, axis=1, keepdims=True) + 1e-6)
    item_emb = (hidden * item_scale * item_gain[...]).astype(bf16)

    wait_dp(hist_buf, hist_send, hist_recv)
    base = (here * item_rows).astype(f32)
    local_rows = iota((item_rows, hist_rows), 0).astype(f32) + base
    wants = []
    for t in range(groups):
        stored = stored_rows(hist_buf[t], parts, item_rows)
        wants.append(jnp.max((local_rows == stored).astype(f32), axis=1, keepdims=True))
    select = slots(wants, item_rows)[:, :rows].astype(bf16)
    outgoing = dot(select, item_emb, 0, 0)
    for t in range(groups):
        emb_out[t] = fold(outgoing[t * CAP : (t + 1) * CAP]).astype(bf16)
    send_dp(lambda peer: emb_out.at[peer], emb_in, emb_send, emb_recv)
    emb_in[here] = emb_out[here]
    wait_dp(emb_in, emb_send, emb_recv)

    x = jnp.concatenate([unfold(emb_in[e].astype(f32)) for e in range(groups)], axis=0)
    scale = lax.rsqrt(jnp.mean(x * x, axis=1, keepdims=True) + 1e-6)
    normed = (x * scale * user_gain[...]).astype(bf16)
    for p in range(chips):
        x_out[p] = normed[:, p * piece : (p + 1) * piece]
    send_chip(lambda mate: x_out.at[mate], x_in, x_send, x_recv)
    x_in[chip] = x_out[chip]

    loads[2].wait()
    w_copy.wait()
    w_all = w_buf[...].reshape(piece, -1)

    wait_chip(sum_buf, sum_send, sum_recv)
    up = dot(sum_buf[...].reshape(chips * rows, -1), w_all, 1, 1)
    up_out[...] = up.reshape(chips, rows, piece)
    send_chip(lambda mate: up_out.at[mate], up_in, up_send, up_recv)
    up_in[chip] = up_out[chip]

    wait_chip(x_in, x_send, x_recv)
    part = dot(x_in[...].reshape(chips * rows, piece), w_all).reshape(chips, rows, -1)
    part_own[...] = part
    part_out[...] = part.astype(bf16)
    send_chip(lambda mate: part_out.at[mate], part_in, part_send, part_recv)

    wait_chip(up_in, up_send, up_recv)
    upstream = jnp.concatenate([up_in[p] for p in range(chips)], axis=1)
    unit = x * scale
    scaled = upstream * user_gain[...]
    block_sum = scale * (scaled - unit * jnp.mean(scaled * unit, axis=1, keepdims=True))
    for t in range(groups):
        back_out[t] = fold(block_sum[t * CAP : (t + 1) * CAP]).astype(bf16)
    send_dp(lambda peer: back_out.at[peer], back_in, back_send, back_recv)
    back_in[here] = back_out[here]

    wait_dp(back_in, back_send, back_recv)
    returned = jnp.concatenate([unfold(back_in[t].astype(f32)) for t in range(groups)], axis=0)
    emb_grad = dot(select, returned.astype(bf16))
    hidden = hidden_buf[...].astype(f32)
    unit = hidden * item_scale
    scaled = emb_grad * item_gain[...]
    item_grad_out[...] = item_scale * (
        scaled - unit * jnp.mean(scaled * unit, axis=1, keepdims=True)
    )

    wait_chip(part_in, part_send, part_recv)
    total = part_own[chip]
    for mate in mates:
        total = total + part_in[mate].astype(f32)
    values_out[...] = dot(place, total.astype(bf16), 0, 0).astype(bf16)

    for copy in sends:
        copy.wait_send()


def local_moving_rows(
    item_hidden, item_gain, history, owner_map, user_gain, value_weight, value_grad
):
    groups = lax.axis_size("dp")
    chips = lax.axis_size("fsdp") // 2
    item_rows, width = item_hidden.shape
    hist_rows, out_width = value_grad.shape
    rows = groups * CAP
    depth = value_weight.shape[0]
    piece = 2 * depth
    vmem = pl.BlockSpec(memory_space=pltpu.VMEM)
    hbm = pl.BlockSpec(memory_space=pl.ANY)

    def dma(count):
        return pltpu.SemaphoreType.DMA((count,))

    return pl.pallas_call(
        functools.partial(kernel, groups, chips),
        out_shape=(
            jax.ShapeDtypeStruct((hist_rows, out_width), bf16),
            jax.ShapeDtypeStruct((item_rows, width), f32),
        ),
        in_specs=[vmem] * 4 + [hbm] * 3,
        out_specs=(vmem, vmem),
        scratch_shapes=[
            pltpu.VMEM((item_rows, width), bf16),
            pltpu.VMEM((hist_rows, out_width), bf16),
            pltpu.VMEM((2, depth, out_width), bf16),
            pltpu.VMEM((groups, 1, hist_rows), jnp.int32),
            pltpu.VMEM((groups, 2 * CAP, width // 2), bf16),
            pltpu.VMEM((groups, 2 * CAP, width // 2), bf16),
            pltpu.VMEM((chips, rows, out_width), bf16),
            pltpu.VMEM((chips, rows, piece), bf16),
            pltpu.VMEM((chips, rows, piece), bf16),
            pltpu.VMEM((chips, rows, out_width), f32),
            pltpu.VMEM((chips, rows, out_width), bf16),
            pltpu.VMEM((chips, rows, out_width), bf16),
            pltpu.VMEM((chips, rows, piece), f32),
            pltpu.VMEM((chips, rows, piece), f32),
            pltpu.VMEM((groups, 2 * CAP, width // 2), bf16),
            pltpu.VMEM((groups, 2 * CAP, width // 2), bf16),
            dma(3), dma(2),
            dma(groups), dma(groups), dma(groups), dma(groups),
            dma(chips), dma(chips), dma(chips), dma(chips),
            dma(chips), dma(chips), dma(chips), dma(chips),
            dma(groups), dma(groups),
        ],
        compiler_params=pltpu.CompilerParams(
            collective_id=0, has_side_effects=True, vmem_limit_bytes=40 * 2**20
        ),
    )(
        item_gain[None, :], history[None, :], owner_map, user_gain[None, :],
        item_hidden, value_weight, value_grad,
    )


def local(item_hidden, item_gain, history, owner_map, user_gain, value_weight, value_grad):
    chips = lax.axis_size("fsdp") // 2
    moved = 2 * chips * lax.axis_size("dp") * CAP
    by_rows = moved <= value_grad.shape[1] and lax.axis_size("dp") * CAP <= 128
    plan = local_moving_rows if by_rows else local_moving_weight
    return plan(
        item_hidden, item_gain, history, owner_map, user_gain, value_weight, value_grad
    )


def solution(mesh):
    in_specs = (
        P(("dp", "fsdp"), None),
        P(),
        P(("dp", "fsdp")),
        P("fsdp", None),
        P(),
        P("fsdp", None),
        P(("dp", "fsdp"), None),
    )
    out_specs = (P(("dp", "fsdp"), None), P(("dp", "fsdp"), None))
    return jax.shard_map(local, mesh=mesh, in_specs=in_specs, out_specs=out_specs, check_vma=False)
```

```python
import functools
import jax
import jax.numpy as jnp
from jax import lax
from jax.experimental import pallas as pl
from jax.experimental.pallas import tpu as pltpu
from jax.sharding import PartitionSpec as P

CAP = 8
MESH = pl.DeviceIdType.MESH
f32 = jnp.float32
bf16 = jnp.bfloat16


eps = 1e-06


def norm_rows(values, gain):
    scale = lax.rsqrt(jnp.mean(values * values, axis=1, keepdims=True) + eps)
    return (values * scale * gain, scale)


def norm_back(values, gain, scale, upstream):
    unit = values * scale
    scaled = upstream * gain
    return scale * (scaled - unit * jnp.mean(scaled * unit, axis=1, keepdims=True))


def locate(owner_row, items):
    matches = items[:, None] == lax.broadcasted_iota(
        jnp.int32, (items.shape[0], owner_row.shape[0]), 1
    )
    return jnp.sum(jnp.where(matches, owner_row[None, :], 0), axis=1)


def local_moving_weight(item_hidden, item_gain, history, owner_map, user_gain, value_weight, value_grad):
    groups = lax.axis_size("dp")
    here = lax.axis_index("dp")
    item_rows = item_hidden.shape[0]
    hist_rows = history.shape[0]
    width = item_hidden.shape[1]
    owner_row = owner_map[0]
    pool = owner_row.shape[0]
    hidden = item_hidden.astype(jnp.float32)
    item_emb, item_scale = norm_rows(hidden, item_gain)
    item_emb = item_emb.astype(jnp.bfloat16)
    all_history = lax.all_gather(history, "dp", axis=0, tiled=True)
    stored_all = locate(owner_row, all_history).reshape(groups, hist_rows)
    local_rows = lax.broadcasted_iota(jnp.int32, (groups, hist_rows, item_rows), 2)
    wanted = jnp.any(stored_all[:, :, None] == here * item_rows + local_rows, axis=1)
    slot = jnp.cumsum(wanted.astype(jnp.int32), axis=1) - 1
    slot_ids = lax.broadcasted_iota(jnp.int32, (groups, CAP, item_rows), 1)
    select = (wanted[:, None, :] & (slot[:, None, :] == slot_ids)).astype(jnp.bfloat16)
    outgoing = jnp.einsum(
        "dcr,rk->dck", select, item_emb, preferred_element_type=jnp.float32
    ).astype(jnp.bfloat16)
    incoming = lax.all_to_all(outgoing, "dp", split_axis=0, concat_axis=0, tiled=True)
    stored = locate(owner_row, history)
    pick = stored[:, None] == lax.broadcasted_iota(jnp.int32, (hist_rows, pool), 1)
    own_wanted = jnp.any(pick, axis=0).reshape(groups, item_rows)
    own_slot = (jnp.cumsum(own_wanted.astype(jnp.int32), axis=1) - 1).reshape(pool)
    slot_pos = jnp.sum(jnp.where(pick, own_slot[None, :], 0), axis=1)
    buffer_row = stored // item_rows * CAP + slot_pos
    x = jnp.take(incoming.reshape(groups * CAP, width), buffer_row, axis=0).astype(jnp.float32)
    normed, scale = norm_rows(x, user_gain)
    normed = normed.astype(jnp.bfloat16)
    whole = lax.all_gather(value_weight, "fsdp", axis=0, tiled=True)
    values = jnp.dot(normed, whole, preferred_element_type=jnp.float32)
    upstream = lax.dot_general(
        value_grad, whole, (((1,), (1,)), ((), ())), preferred_element_type=jnp.float32
    )
    values = values.astype(jnp.bfloat16)
    dx = norm_back(x, user_gain, scale, upstream)
    one_hot = (
        buffer_row[:, None] == lax.broadcasted_iota(jnp.int32, (hist_rows, groups * CAP), 1)
    ).astype(jnp.float32)
    summed = lax.dot_general(
        one_hot,
        dx,
        (((0,), (0,)), ((), ())),
        precision=lax.Precision.HIGHEST,
        preferred_element_type=jnp.float32,
    )
    returned = lax.all_to_all(
        summed.astype(jnp.bfloat16).reshape(groups, CAP, width),
        "dp",
        split_axis=0,
        concat_axis=0,
        tiled=True,
    )
    emb_grad = jnp.einsum("dcr,dck->rk", select, returned, preferred_element_type=jnp.float32)
    item_grad = norm_back(hidden, item_gain, item_scale, emb_grad)
    return (values, item_grad)


def iota(shape, dim):
    return lax.broadcasted_iota(jnp.int32, shape, dim)


def dot(a, b, ca=1, cb=0):
    return lax.dot_general(a, b, (((ca,), (cb,)), ((), ())), preferred_element_type=f32)


def fold(rows):
    half = rows.shape[1] // 2
    return jnp.concatenate([rows[:, :half], rows[:, half:]], axis=0)


def unfold(rows):
    return jnp.concatenate([rows[:CAP], rows[CAP:]], axis=1)


def stored_rows(hist, parts, item_rows):
    pool = parts.shape[1]
    named = (iota((pool, hist.shape[1]), 0) == hist).astype(f32).astype(bf16)
    found = dot(parts, named)
    return found[0:1] * item_rows + found[1:2]


def slots(wants, item_rows):
    lane = iota((item_rows, 128), 1)
    wanted = jnp.zeros((item_rows, 128), f32)
    for group, want in enumerate(wants):
        wanted = jnp.where(lane // CAP == group, want, wanted)
    before = (iota((item_rows, item_rows), 1) < iota((item_rows, item_rows), 0)).astype(f32)
    slot = dot(before.astype(bf16), wanted.astype(bf16))
    return jnp.where(slot == (lane % CAP).astype(f32), wanted, 0.0)


def kernel(
    groups, chips,
    item_gain_hbm, history_hbm, owner_hbm, user_gain_hbm, item_hidden, weight, value_grad,
    back_in, total_out, place_out, select_out,
    item_gain, history, owner, user_gain,
    hidden_buf, grad_buf, w_buf, hist_buf, emb_out, emb_in, sum_buf, x_out, x_in,
    part_own, part_out, part_in, up_out, up_in, back_out, total_buf, place_buf, select_buf,
    local_sem, out_sem, w_sem, hello, hist_send, hist_recv, emb_send, emb_recv, sum_send, sum_recv,
    x_send, x_recv, part_send, part_recv, up_send, up_recv, back_send, back_recv,
):
    here = lax.axis_index("dp")
    fsdp = lax.axis_index("fsdp")
    chip = fsdp // 2
    core = fsdp % 2
    item_rows, width = item_hidden.shape
    hist_rows = history.shape[1]
    rows = groups * CAP
    piece = width // chips
    peers = [lax.rem(here + k, groups) for k in range(1, groups)]
    mates = [lax.rem(chip + k, chips) for k in range(1, chips)]

    def dp_id(peer):
        return (peer, fsdp)

    def chip_id(mate):
        return (here, mate * 2 + core)

    sibling = (here, chip * 2 + 1 - core)

    barrier = pltpu.get_barrier_semaphore()
    group = [dp_id(p) for p in peers] + [chip_id(m) for m in mates]
    for target in group:
        pl.semaphore_signal(barrier, inc=1, device_id=target, device_id_type=MESH)

    loads = [
        pltpu.make_async_copy(src, dst, local_sem.at[k])
        for k, (src, dst) in enumerate([
            (history_hbm, history), (owner_hbm, owner), (value_grad, grad_buf),
            (item_hidden, hidden_buf), (item_gain_hbm, item_gain),
            (user_gain_hbm, user_gain), (weight, w_buf.at[core]),
        ])
    ]
    for load in loads:
        load.start()

    @pl.when(core == 0)
    def _():
        pl.semaphore_wait(barrier, len(group))
        pl.semaphore_signal(barrier, inc=1, device_id=sibling, device_id_type=MESH)

    @pl.when(core == 1)
    def _():
        pl.semaphore_wait(barrier, len(group) + 1)
        pl.semaphore_signal(hello, inc=1, device_id=sibling, device_id_type=MESH)

    def remote(src, dst, send, recv, target):
        return pltpu.make_async_remote_copy(
            src_ref=src, dst_ref=dst, send_sem=send, recv_sem=recv,
            device_id=target, device_id_type=MESH,
        )

    sends = []

    def send_dp(out_of, into, send, recv):
        for k, peer in enumerate(peers):
            copy = remote(out_of(peer), into.at[here], send.at[k], recv.at[here], dp_id(peer))
            copy.start()
            sends.append(copy)

    def wait_dp(into, send, recv):
        for k, peer in enumerate(peers):
            remote(into.at[peer], into.at[peer], send.at[k], recv.at[peer], dp_id(peer)).wait_recv()

    def send_chip(out_of, into, send, recv):
        for k, mate in enumerate(mates):
            copy = remote(out_of(mate), into.at[chip], send.at[k], recv.at[chip], chip_id(mate))
            copy.start()
            sends.append(copy)

    def wait_chip(into, send, recv):
        for k, mate in enumerate(mates):
            remote(into.at[mate], into.at[mate], send.at[k], recv.at[mate], chip_id(mate)).wait_recv()

    loads[0].wait()
    send_dp(lambda peer: history, hist_buf, hist_send, hist_recv)
    hist_buf[here] = history[...]

    loads[1].wait()
    owner_row = owner[...]
    pool = owner_row.shape[1]
    div = (owner_row // item_rows).astype(f32)
    mod = (owner_row % item_rows).astype(f32)
    parts = jnp.where(iota((8, pool), 0) == 0, div, mod).astype(bf16)

    own = stored_rows(history[...], parts, item_rows)
    match = (iota((pool, hist_rows), 0).astype(f32) == own).astype(f32)
    wants = [
        jnp.max(match[e * item_rows : (e + 1) * item_rows], axis=1, keepdims=True)
        for e in range(groups)
    ]
    one_hot = slots(wants, item_rows)
    lane = iota((item_rows, 128), 1)
    stacked = jnp.concatenate(
        [jnp.where(lane // CAP == e, one_hot, 0.0) for e in range(groups)], axis=0
    )
    place = dot(stacked.astype(bf16), match.astype(bf16), 0, 0)[:rows]
    place = place.astype(bf16)
    place_buf[...] = place
    outs = [pltpu.make_async_copy(place_buf, place_out, out_sem.at[0])]
    outs[0].start()

    loads[2].wait()
    sum_buf[chip] = dot(place, grad_buf[...]).astype(bf16)
    send_chip(lambda mate: sum_buf.at[chip], sum_buf, sum_send, sum_recv)

    w_copy = remote(weight, w_buf.at[core], w_sem.at[0], w_sem.at[1], sibling)

    @pl.when(core == 1)
    def _():
        w_copy.start()

    loads[3].wait()
    loads[4].wait()
    hidden = hidden_buf[...].astype(f32)
    item_scale = lax.rsqrt(jnp.mean(hidden * hidden, axis=1, keepdims=True) + 1e-6)
    item_emb = (hidden * item_scale * item_gain[...]).astype(bf16)

    wait_dp(hist_buf, hist_send, hist_recv)
    base = (here * item_rows).astype(f32)
    local_rows = iota((item_rows, hist_rows), 0).astype(f32) + base
    wants = []
    for t in range(groups):
        stored = stored_rows(hist_buf[t], parts, item_rows)
        wants.append(jnp.max((local_rows == stored).astype(f32), axis=1, keepdims=True))
    select = slots(wants, item_rows)[:, :rows].astype(bf16)
    select_buf[...] = select
    outs.append(pltpu.make_async_copy(select_buf, select_out, out_sem.at[1]))
    outs[1].start()
    outgoing = dot(select, item_emb, 0, 0)
    for t in range(groups):
        emb_out[t] = fold(outgoing[t * CAP : (t + 1) * CAP]).astype(bf16)
    send_dp(lambda peer: emb_out.at[peer], emb_in, emb_send, emb_recv)
    emb_in[here] = emb_out[here]

    @pl.when(core == 0)
    def _():
        pl.semaphore_wait(hello, 1)
        w_copy.start()

    loads[5].wait()
    wait_dp(emb_in, emb_send, emb_recv)

    x = jnp.concatenate([unfold(emb_in[e].astype(f32)) for e in range(groups)], axis=0)
    scale = lax.rsqrt(jnp.mean(x * x, axis=1, keepdims=True) + 1e-6)
    normed = (x * scale * user_gain[...]).astype(bf16)
    for p in range(chips):
        x_out[p] = normed[:, p * piece : (p + 1) * piece]
    send_chip(lambda mate: x_out.at[mate], x_in, x_send, x_recv)
    x_in[chip] = x_out[chip]

    loads[6].wait()
    w_copy.wait()
    w_all = w_buf[...].reshape(piece, -1)

    wait_chip(sum_buf, sum_send, sum_recv)
    up = dot(sum_buf[...].reshape(chips * rows, -1), w_all, 1, 1)
    up_out[...] = up.reshape(chips, rows, piece)
    send_chip(lambda mate: up_out.at[mate], up_in, up_send, up_recv)
    up_in[chip] = up_out[chip]

    wait_chip(x_in, x_send, x_recv)
    part = dot(x_in[...].reshape(chips * rows, piece), w_all).reshape(chips, rows, -1)
    part_own[...] = part
    part_out[...] = part.astype(bf16)
    send_chip(lambda mate: part_out.at[mate], part_in, part_send, part_recv)

    wait_chip(up_in, up_send, up_recv)
    upstream = jnp.concatenate([up_in[p] for p in range(chips)], axis=1)
    unit = x * scale
    scaled = upstream * user_gain[...]
    block_sum = scale * (scaled - unit * jnp.mean(scaled * unit, axis=1, keepdims=True))
    for t in range(groups):
        back_out[t] = fold(block_sum[t * CAP : (t + 1) * CAP]).astype(bf16)
    send_dp(lambda peer: back_out.at[peer], back_in, back_send, back_recv)
    outs.append(pltpu.make_async_copy(back_out.at[here], back_in.at[here], out_sem.at[2]))
    outs[2].start()

    wait_chip(part_in, part_send, part_recv)
    total = part_own[chip]
    for mate in mates:
        total = total + part_in[mate].astype(f32)
    total_buf[...] = total.astype(bf16)
    outs.append(pltpu.make_async_copy(total_buf, total_out, out_sem.at[3]))
    outs[3].start()

    wait_dp(back_in, back_send, back_recv)
    for out in outs:
        out.wait()
    for copy in sends:
        copy.wait_send()


def finish(
    groups, back_hbm, total_hbm, place_hbm, select_hbm, hidden_hbm, gain_hbm,
    values_out, item_grad_out,
    back, total, place, select, hidden_buf, gain, values, item_grad, load_sem, out_sem,
):
    loads = [
        pltpu.make_async_copy(src, dst, load_sem.at[k])
        for k, (src, dst) in enumerate([
            (hidden_hbm, hidden_buf), (gain_hbm, gain), (select_hbm, select), (back_hbm, back),
            (place_hbm, place), (total_hbm, total),
        ])
    ]
    for load in loads:
        load.start()
    for load in loads[:4]:
        load.wait()
    hidden = hidden_buf[...].astype(f32)
    scale = lax.rsqrt(jnp.mean(hidden * hidden, axis=1, keepdims=True) + 1e-6)
    returned = jnp.concatenate([unfold(back[t].astype(f32)) for t in range(groups)], axis=0)
    emb_grad = dot(select[...], returned.astype(bf16))
    unit = hidden * scale
    scaled = emb_grad * gain[...]
    item_grad[...] = scale * (scaled - unit * jnp.mean(scaled * unit, axis=1, keepdims=True))
    grad_copy = pltpu.make_async_copy(item_grad, item_grad_out, out_sem.at[0])
    grad_copy.start()
    loads[4].wait()
    loads[5].wait()
    values[...] = dot(place[...], total[...], 0, 0).astype(bf16)
    values_copy = pltpu.make_async_copy(values, values_out, out_sem.at[1])
    values_copy.start()
    grad_copy.wait()
    values_copy.wait()


def local_moving_rows(
    item_hidden, item_gain, history, owner_map, user_gain, value_weight, value_grad
):
    groups = lax.axis_size("dp")
    chips = lax.axis_size("fsdp") // 2
    item_rows, width = item_hidden.shape
    hist_rows, out_width = value_grad.shape
    rows = groups * CAP
    depth = value_weight.shape[0]
    piece = 2 * depth
    hbm = pl.BlockSpec(memory_space=pl.ANY)

    def dma(count):
        return pltpu.SemaphoreType.DMA((count,))

    folded = (groups, 2 * CAP, width // 2)
    back, total, place, select = pl.pallas_call(
        functools.partial(kernel, groups, chips),
        out_shape=(
            jax.ShapeDtypeStruct(folded, bf16),
            jax.ShapeDtypeStruct((rows, out_width), bf16),
            jax.ShapeDtypeStruct((rows, hist_rows), bf16),
            jax.ShapeDtypeStruct((item_rows, rows), bf16),
        ),
        in_specs=[hbm] * 7,
        out_specs=(hbm,) * 4,
        scratch_shapes=[
            pltpu.VMEM((1, width), f32),
            pltpu.VMEM((1, hist_rows), jnp.int32),
            pltpu.VMEM((1, owner_map.shape[1]), jnp.int32),
            pltpu.VMEM((1, width), f32),
            pltpu.VMEM((item_rows, width), bf16),
            pltpu.VMEM((hist_rows, out_width), bf16),
            pltpu.VMEM((2, depth, out_width), bf16),
            pltpu.VMEM((groups, 1, hist_rows), jnp.int32),
            pltpu.VMEM(folded, bf16),
            pltpu.VMEM(folded, bf16),
            pltpu.VMEM((chips, rows, out_width), bf16),
            pltpu.VMEM((chips, rows, piece), bf16),
            pltpu.VMEM((chips, rows, piece), bf16),
            pltpu.VMEM((chips, rows, out_width), f32),
            pltpu.VMEM((chips, rows, out_width), bf16),
            pltpu.VMEM((chips, rows, out_width), bf16),
            pltpu.VMEM((chips, rows, piece), f32),
            pltpu.VMEM((chips, rows, piece), f32),
            pltpu.VMEM(folded, bf16),
            pltpu.VMEM((rows, out_width), bf16),
            pltpu.VMEM((rows, hist_rows), bf16),
            pltpu.VMEM((item_rows, rows), bf16),
            dma(7), dma(4), dma(2), pltpu.SemaphoreType.REGULAR,
            dma(groups), dma(groups), dma(groups), dma(groups),
            dma(chips), dma(chips), dma(chips), dma(chips),
            dma(chips), dma(chips), dma(chips), dma(chips),
            dma(groups), dma(groups),
        ],
        compiler_params=pltpu.CompilerParams(
            collective_id=0, has_side_effects=True, vmem_limit_bytes=60 * 2**20
        ),
    )(
        item_gain[None, :], history[None, :], owner_map, user_gain[None, :],
        item_hidden, value_weight, value_grad,
    )
    return pl.pallas_call(
        functools.partial(finish, groups),
        out_shape=(
            jax.ShapeDtypeStruct((hist_rows, out_width), bf16),
            jax.ShapeDtypeStruct((item_rows, width), f32),
        ),
        in_specs=[hbm] * 6,
        out_specs=(hbm,) * 2,
        scratch_shapes=[
            pltpu.VMEM(folded, bf16),
            pltpu.VMEM((rows, out_width), bf16),
            pltpu.VMEM((rows, hist_rows), bf16),
            pltpu.VMEM((item_rows, rows), bf16),
            pltpu.VMEM((item_rows, width), bf16),
            pltpu.VMEM((1, width), f32),
            pltpu.VMEM((hist_rows, out_width), bf16),
            pltpu.VMEM((item_rows, width), f32),
            dma(6), dma(2),
        ],
        compiler_params=pltpu.CompilerParams(vmem_limit_bytes=60 * 2**20),
    )(back, total, place, select, item_hidden, item_gain[None, :])


def local(item_hidden, item_gain, history, owner_map, user_gain, value_weight, value_grad):
    chips = lax.axis_size("fsdp") // 2
    moved = 2 * chips * lax.axis_size("dp") * CAP
    by_rows = moved <= value_grad.shape[1] and lax.axis_size("dp") * CAP <= 128
    plan = local_moving_rows if by_rows else local_moving_weight
    return plan(
        item_hidden, item_gain, history, owner_map, user_gain, value_weight, value_grad
    )


def solution(mesh):
    in_specs = (
        P(("dp", "fsdp"), None),
        P(),
        P(("dp", "fsdp")),
        P("fsdp", None),
        P(),
        P("fsdp", None),
        P(("dp", "fsdp"), None),
    )
    out_specs = (P(("dp", "fsdp"), None), P(("dp", "fsdp"), None))
    return jax.shard_map(local, mesh=mesh, in_specs=in_specs, out_specs=out_specs, check_vma=False)
```

```python
import functools
import jax
import jax.numpy as jnp
from jax import lax
from jax.experimental import pallas as pl
from jax.experimental.pallas import tpu as pltpu
from jax.sharding import PartitionSpec as P

CAP = 8
MESH = pl.DeviceIdType.MESH
f32 = jnp.float32
bf16 = jnp.bfloat16


eps = 1e-06


def norm_rows(values, gain):
    scale = lax.rsqrt(jnp.mean(values * values, axis=1, keepdims=True) + eps)
    return (values * scale * gain, scale)


def norm_back(values, gain, scale, upstream):
    unit = values * scale
    scaled = upstream * gain
    return scale * (scaled - unit * jnp.mean(scaled * unit, axis=1, keepdims=True))


def locate(owner_row, items):
    matches = items[:, None] == lax.broadcasted_iota(
        jnp.int32, (items.shape[0], owner_row.shape[0]), 1
    )
    return jnp.sum(jnp.where(matches, owner_row[None, :], 0), axis=1)


def local_moving_weight(item_hidden, item_gain, history, owner_map, user_gain, value_weight, value_grad):
    groups = lax.axis_size("dp")
    here = lax.axis_index("dp")
    item_rows = item_hidden.shape[0]
    hist_rows = history.shape[0]
    width = item_hidden.shape[1]
    owner_row = owner_map[0]
    pool = owner_row.shape[0]
    hidden = item_hidden.astype(jnp.float32)
    item_emb, item_scale = norm_rows(hidden, item_gain)
    item_emb = item_emb.astype(jnp.bfloat16)
    all_history = lax.all_gather(history, "dp", axis=0, tiled=True)
    stored_all = locate(owner_row, all_history).reshape(groups, hist_rows)
    local_rows = lax.broadcasted_iota(jnp.int32, (groups, hist_rows, item_rows), 2)
    wanted = jnp.any(stored_all[:, :, None] == here * item_rows + local_rows, axis=1)
    slot = jnp.cumsum(wanted.astype(jnp.int32), axis=1) - 1
    slot_ids = lax.broadcasted_iota(jnp.int32, (groups, CAP, item_rows), 1)
    select = (wanted[:, None, :] & (slot[:, None, :] == slot_ids)).astype(jnp.bfloat16)
    outgoing = jnp.einsum(
        "dcr,rk->dck", select, item_emb, preferred_element_type=jnp.float32
    ).astype(jnp.bfloat16)
    incoming = lax.all_to_all(outgoing, "dp", split_axis=0, concat_axis=0, tiled=True)
    stored = locate(owner_row, history)
    pick = stored[:, None] == lax.broadcasted_iota(jnp.int32, (hist_rows, pool), 1)
    own_wanted = jnp.any(pick, axis=0).reshape(groups, item_rows)
    own_slot = (jnp.cumsum(own_wanted.astype(jnp.int32), axis=1) - 1).reshape(pool)
    slot_pos = jnp.sum(jnp.where(pick, own_slot[None, :], 0), axis=1)
    buffer_row = stored // item_rows * CAP + slot_pos
    x = jnp.take(incoming.reshape(groups * CAP, width), buffer_row, axis=0).astype(jnp.float32)
    normed, scale = norm_rows(x, user_gain)
    normed = normed.astype(jnp.bfloat16)
    whole = lax.all_gather(value_weight, "fsdp", axis=0, tiled=True)
    values = jnp.dot(normed, whole, preferred_element_type=jnp.float32)
    upstream = lax.dot_general(
        value_grad, whole, (((1,), (1,)), ((), ())), preferred_element_type=jnp.float32
    )
    values = values.astype(jnp.bfloat16)
    dx = norm_back(x, user_gain, scale, upstream)
    one_hot = (
        buffer_row[:, None] == lax.broadcasted_iota(jnp.int32, (hist_rows, groups * CAP), 1)
    ).astype(jnp.float32)
    summed = lax.dot_general(
        one_hot,
        dx,
        (((0,), (0,)), ((), ())),
        precision=lax.Precision.HIGHEST,
        preferred_element_type=jnp.float32,
    )
    returned = lax.all_to_all(
        summed.astype(jnp.bfloat16).reshape(groups, CAP, width),
        "dp",
        split_axis=0,
        concat_axis=0,
        tiled=True,
    )
    emb_grad = jnp.einsum("dcr,dck->rk", select, returned, preferred_element_type=jnp.float32)
    item_grad = norm_back(hidden, item_gain, item_scale, emb_grad)
    return (values, item_grad)


CHUNKS = 4


def iota(shape, dim):
    return lax.broadcasted_iota(jnp.int32, shape, dim)


def dot(a, b, ca=1, cb=0):
    return lax.dot_general(a, b, (((ca,), (cb,)), ((), ())), preferred_element_type=f32)


def fold(rows):
    half = rows.shape[1] // 2
    return jnp.concatenate([rows[:, :half], rows[:, half:]], axis=0)


def unfold(rows):
    return jnp.concatenate([rows[:CAP], rows[CAP:]], axis=1)


def stored_rows(hist, parts, item_rows):
    pool = parts.shape[1]
    named = (iota((pool, hist.shape[1]), 0) == hist).astype(f32).astype(bf16)
    found = dot(parts, named)
    return found[0:1] * item_rows + found[1:2]


def slots(wants, item_rows):
    lane = iota((item_rows, 128), 1)
    wanted = jnp.zeros((item_rows, 128), f32)
    for group, want in enumerate(wants):
        wanted = jnp.where(lane // CAP == group, want, wanted)
    before = (iota((item_rows, item_rows), 1) < iota((item_rows, item_rows), 0)).astype(f32)
    slot = dot(before.astype(bf16), wanted.astype(bf16))
    return jnp.where(slot == (lane % CAP).astype(f32), wanted, 0.0)


def kernel(
    groups, chips,
    item_gain_hbm, history_hbm, owner_hbm, user_gain_hbm, item_hidden, weight, value_grad,
    back_in, total_out, place_out, select_out,
    item_gain, history, owner, user_gain,
    hidden_buf, grad_buf, w_buf, hist_buf, emb_out, emb_in, sum_buf, x_out, x_in,
    part_own, part_out, part_in, up_out, up_in, back_out, total_buf, place_buf, select_buf,
    local_sem, out_sem, w_sem, hello, hist_send, hist_recv, emb_send, emb_recv, sum_send, sum_recv,
    x_send, x_recv, part_send, part_recv, up_send, up_recv, back_send, back_recv,
):
    here = lax.axis_index("dp")
    fsdp = lax.axis_index("fsdp")
    chip = fsdp // 2
    core = fsdp % 2
    item_rows, width = item_hidden.shape
    hist_rows = history.shape[1]
    rows = groups * CAP
    piece = width // chips
    cols = value_grad.shape[1] // CHUNKS
    peers = [lax.rem(here + k, groups) for k in range(1, groups)]
    mates = [lax.rem(chip + k, chips) for k in range(1, chips)]

    def dp_id(peer):
        return (peer, fsdp)

    def chip_id(mate):
        return (here, mate * 2 + core)

    sibling = (here, chip * 2 + 1 - core)

    barrier = pltpu.get_barrier_semaphore()
    group = [dp_id(p) for p in peers] + [chip_id(m) for m in mates]
    for target in group:
        pl.semaphore_signal(barrier, inc=1, device_id=target, device_id_type=MESH)

    loads = [
        pltpu.make_async_copy(src, dst, local_sem.at[k])
        for k, (src, dst) in enumerate([
            (history_hbm, history), (owner_hbm, owner), (value_grad, grad_buf),
            (item_hidden, hidden_buf), (item_gain_hbm, item_gain),
            (user_gain_hbm, user_gain), (weight, w_buf.at[core]),
        ])
    ]
    for load in loads:
        load.start()

    @pl.when(core == 0)
    def _():
        pl.semaphore_wait(barrier, len(group))
        pl.semaphore_signal(barrier, inc=1, device_id=sibling, device_id_type=MESH)

    @pl.when(core == 1)
    def _():
        pl.semaphore_wait(barrier, len(group) + 1)
        pl.semaphore_signal(hello, inc=1, device_id=sibling, device_id_type=MESH)

    w_copy = pltpu.make_async_remote_copy(
        src_ref=weight, dst_ref=w_buf.at[core], send_sem=w_sem.at[0], recv_sem=w_sem.at[1],
        device_id=sibling, device_id_type=MESH,
    )

    @pl.when(core == 1)
    def _():
        w_copy.start()

    def remote(src, dst, send, recv, target):
        return pltpu.make_async_remote_copy(
            src_ref=src, dst_ref=dst, send_sem=send, recv_sem=recv,
            device_id=target, device_id_type=MESH,
        )

    sends = []

    def send_dp(out_of, into, send, recv):
        for k, peer in enumerate(peers):
            copy = remote(out_of(peer), into.at[here], send.at[k], recv.at[here], dp_id(peer))
            copy.start()
            sends.append(copy)

    def wait_dp(into, send, recv):
        for k, peer in enumerate(peers):
            remote(into.at[peer], into.at[peer], send.at[k], recv.at[peer], dp_id(peer)).wait_recv()

    def send_chip(out_of, into, send, recv):
        for k, mate in enumerate(mates):
            copy = remote(out_of(mate), into.at[chip], send.at[k], recv.at[chip], chip_id(mate))
            copy.start()
            sends.append(copy)

    def wait_chip(into, send, recv):
        for k, mate in enumerate(mates):
            remote(into.at[mate], into.at[mate], send.at[k], recv.at[mate], chip_id(mate)).wait_recv()

    loads[0].wait()
    send_dp(lambda peer: history, hist_buf, hist_send, hist_recv)
    hist_buf[here] = history[...]

    loads[1].wait()
    owner_row = owner[...]
    pool = owner_row.shape[1]
    div = (owner_row // item_rows).astype(f32)
    mod = (owner_row % item_rows).astype(f32)
    parts = jnp.where(iota((8, pool), 0) == 0, div, mod).astype(bf16)

    own = stored_rows(history[...], parts, item_rows)
    match = (iota((pool, hist_rows), 0).astype(f32) == own).astype(f32)
    wants = [
        jnp.max(match[e * item_rows : (e + 1) * item_rows], axis=1, keepdims=True)
        for e in range(groups)
    ]
    one_hot = slots(wants, item_rows)
    lane = iota((item_rows, 128), 1)
    stacked = jnp.concatenate(
        [jnp.where(lane // CAP == e, one_hot, 0.0) for e in range(groups)], axis=0
    )
    place = dot(stacked.astype(bf16), match.astype(bf16), 0, 0)[:rows]
    place = place.astype(bf16)
    place_buf[...] = place
    outs = [pltpu.make_async_copy(place_buf, place_out, out_sem.at[0])]
    outs[0].start()

    loads[2].wait()
    for c in range(CHUNKS):
        sum_buf[c, chip] = dot(place, grad_buf[:, c * cols : (c + 1) * cols]).astype(bf16)
        send_chip(
            lambda mate: sum_buf.at[c, chip], sum_buf.at[c], sum_send.at[c], sum_recv.at[c]
        )

    loads[3].wait()
    loads[4].wait()
    hidden = hidden_buf[...].astype(f32)
    item_scale = lax.rsqrt(jnp.mean(hidden * hidden, axis=1, keepdims=True) + 1e-6)
    item_emb = (hidden * item_scale * item_gain[...]).astype(bf16)

    wait_dp(hist_buf, hist_send, hist_recv)
    base = (here * item_rows).astype(f32)
    local_rows = iota((item_rows, hist_rows), 0).astype(f32) + base
    wants = []
    for t in range(groups):
        stored = stored_rows(hist_buf[t], parts, item_rows)
        wants.append(jnp.max((local_rows == stored).astype(f32), axis=1, keepdims=True))
    select = slots(wants, item_rows)[:, :rows].astype(bf16)
    select_buf[...] = select
    outs.append(pltpu.make_async_copy(select_buf, select_out, out_sem.at[1]))
    outs[1].start()
    outgoing = dot(select, item_emb, 0, 0)
    for t in range(groups):
        emb_out[t] = fold(outgoing[t * CAP : (t + 1) * CAP]).astype(bf16)
    send_dp(lambda peer: emb_out.at[peer], emb_in, emb_send, emb_recv)
    emb_in[here] = emb_out[here]

    @pl.when(core == 0)
    def _():
        pl.semaphore_wait(hello, 1)
        w_copy.start()

    loads[5].wait()
    wait_dp(emb_in, emb_send, emb_recv)

    x = jnp.concatenate([unfold(emb_in[e].astype(f32)) for e in range(groups)], axis=0)
    scale = lax.rsqrt(jnp.mean(x * x, axis=1, keepdims=True) + 1e-6)
    normed = (x * scale * user_gain[...]).astype(bf16)
    for p in range(chips):
        x_out[p] = normed[:, p * piece : (p + 1) * piece]
    send_chip(lambda mate: x_out.at[mate], x_in, x_send, x_recv)
    x_in[chip] = x_out[chip]

    loads[6].wait()
    w_copy.wait()
    w_all = w_buf[...].reshape(piece, -1)

    up = jnp.zeros((chips * rows, piece), f32)
    for c in range(CHUNKS):
        wait_chip(sum_buf.at[c], sum_send.at[c], sum_recv.at[c])
        sums = sum_buf[c].reshape(chips * rows, cols)
        up = up + dot(sums, w_all[:, c * cols : (c + 1) * cols], 1, 1)
    up_out[...] = up.reshape(chips, rows, piece)
    send_chip(lambda mate: up_out.at[mate], up_in, up_send, up_recv)
    up_in[chip] = up_out[chip]

    wait_chip(x_in, x_send, x_recv)
    x_all = x_in[...].reshape(chips * rows, piece)
    for c in range(CHUNKS):
        part = dot(x_all, w_all[:, c * cols : (c + 1) * cols]).reshape(chips, rows, cols)
        part_own[c] = part
        part_out[c] = part.astype(bf16)
        send_chip(
            lambda mate: part_out.at[c, mate], part_in.at[c], part_send.at[c], part_recv.at[c]
        )

    wait_chip(up_in, up_send, up_recv)
    upstream = jnp.concatenate([up_in[p] for p in range(chips)], axis=1)
    unit = x * scale
    scaled = upstream * user_gain[...]
    block_sum = scale * (scaled - unit * jnp.mean(scaled * unit, axis=1, keepdims=True))
    for t in range(groups):
        back_out[t] = fold(block_sum[t * CAP : (t + 1) * CAP]).astype(bf16)
    send_dp(lambda peer: back_out.at[peer], back_in, back_send, back_recv)
    outs.append(pltpu.make_async_copy(back_out.at[here], back_in.at[here], out_sem.at[2]))
    outs[2].start()

    for c in range(CHUNKS):
        wait_chip(part_in.at[c], part_send.at[c], part_recv.at[c])
        total = part_own[c, chip]
        for mate in mates:
            total = total + part_in[c, mate].astype(f32)
        total_buf[c] = total.astype(bf16)
        out = pltpu.make_async_copy(total_buf.at[c], total_out.at[c], out_sem.at[3 + c])
        out.start()
        outs.append(out)

    wait_dp(back_in, back_send, back_recv)
    for out in outs:
        out.wait()
    for copy in sends:
        copy.wait_send()


def finish(
    groups, back_hbm, total_hbm, place_hbm, select_hbm, hidden_hbm, gain_hbm,
    values_out, item_grad_out,
    back, total, place, select, hidden_buf, gain, values, item_grad, load_sem, out_sem,
):
    loads = [
        pltpu.make_async_copy(src, dst, load_sem.at[k])
        for k, (src, dst) in enumerate([
            (hidden_hbm, hidden_buf), (gain_hbm, gain), (select_hbm, select), (back_hbm, back),
            (place_hbm, place), (total_hbm, total),
        ])
    ]
    for load in loads:
        load.start()
    loads[0].wait()
    loads[1].wait()
    hidden = hidden_buf[...].astype(f32)
    scale = lax.rsqrt(jnp.mean(hidden * hidden, axis=1, keepdims=True) + 1e-6)
    loads[2].wait()
    loads[3].wait()
    returned = jnp.concatenate([unfold(back[t].astype(f32)) for t in range(groups)], axis=0)
    emb_grad = dot(select[...], returned.astype(bf16))
    unit = hidden * scale
    scaled = emb_grad * gain[...]
    item_grad[...] = scale * (scaled - unit * jnp.mean(scaled * unit, axis=1, keepdims=True))
    grad_copy = pltpu.make_async_copy(item_grad, item_grad_out, out_sem.at[0])
    grad_copy.start()
    loads[4].wait()
    loads[5].wait()
    named = place[...]
    cols = total.shape[2]
    for c in range(CHUNKS):
        values[:, c * cols : (c + 1) * cols] = dot(named, total[c], 0, 0).astype(bf16)
    values_copy = pltpu.make_async_copy(values, values_out, out_sem.at[1])
    values_copy.start()
    grad_copy.wait()
    values_copy.wait()


def local_moving_rows(
    item_hidden, item_gain, history, owner_map, user_gain, value_weight, value_grad
):
    groups = lax.axis_size("dp")
    chips = lax.axis_size("fsdp") // 2
    item_rows, width = item_hidden.shape
    hist_rows, out_width = value_grad.shape
    rows = groups * CAP
    depth = value_weight.shape[0]
    piece = 2 * depth
    cols = out_width // CHUNKS
    hbm = pl.BlockSpec(memory_space=pl.ANY)

    def dma(*counts):
        return pltpu.SemaphoreType.DMA(counts)

    folded = (groups, 2 * CAP, width // 2)
    back, total, place, select = pl.pallas_call(
        functools.partial(kernel, groups, chips),
        out_shape=(
            jax.ShapeDtypeStruct(folded, bf16),
            jax.ShapeDtypeStruct((CHUNKS, rows, cols), bf16),
            jax.ShapeDtypeStruct((rows, hist_rows), bf16),
            jax.ShapeDtypeStruct((item_rows, rows), bf16),
        ),
        in_specs=[hbm] * 7,
        out_specs=(hbm,) * 4,
        scratch_shapes=[
            pltpu.VMEM((1, width), f32),
            pltpu.VMEM((1, hist_rows), jnp.int32),
            pltpu.VMEM((1, owner_map.shape[1]), jnp.int32),
            pltpu.VMEM((1, width), f32),
            pltpu.VMEM((item_rows, width), bf16),
            pltpu.VMEM((hist_rows, out_width), bf16),
            pltpu.VMEM((2, depth, out_width), bf16),
            pltpu.VMEM((groups, 1, hist_rows), jnp.int32),
            pltpu.VMEM(folded, bf16),
            pltpu.VMEM(folded, bf16),
            pltpu.VMEM((CHUNKS, chips, rows, cols), bf16),
            pltpu.VMEM((chips, rows, piece), bf16),
            pltpu.VMEM((chips, rows, piece), bf16),
            pltpu.VMEM((CHUNKS, chips, rows, cols), f32),
            pltpu.VMEM((CHUNKS, chips, rows, cols), bf16),
            pltpu.VMEM((CHUNKS, chips, rows, cols), bf16),
            pltpu.VMEM((chips, rows, piece), f32),
            pltpu.VMEM((chips, rows, piece), f32),
            pltpu.VMEM(folded, bf16),
            pltpu.VMEM((CHUNKS, rows, cols), bf16),
            pltpu.VMEM((rows, hist_rows), bf16),
            pltpu.VMEM((item_rows, rows), bf16),
            dma(7), dma(3 + CHUNKS), dma(2), pltpu.SemaphoreType.REGULAR,
            dma(groups), dma(groups), dma(groups), dma(groups),
            dma(CHUNKS, chips), dma(CHUNKS, chips), dma(chips), dma(chips),
            dma(CHUNKS, chips), dma(CHUNKS, chips), dma(chips), dma(chips),
            dma(groups), dma(groups),
        ],
        compiler_params=pltpu.CompilerParams(
            collective_id=0, has_side_effects=True, vmem_limit_bytes=60 * 2**20
        ),
    )(
        item_gain[None, :], history[None, :], owner_map, user_gain[None, :],
        item_hidden, value_weight, value_grad,
    )
    return pl.pallas_call(
        functools.partial(finish, groups),
        out_shape=(
            jax.ShapeDtypeStruct((hist_rows, out_width), bf16),
            jax.ShapeDtypeStruct((item_rows, width), f32),
        ),
        in_specs=[hbm] * 6,
        out_specs=(hbm,) * 2,
        scratch_shapes=[
            pltpu.VMEM(folded, bf16),
            pltpu.VMEM((CHUNKS, rows, cols), bf16),
            pltpu.VMEM((rows, hist_rows), bf16),
            pltpu.VMEM((item_rows, rows), bf16),
            pltpu.VMEM((item_rows, width), bf16),
            pltpu.VMEM((1, width), f32),
            pltpu.VMEM((hist_rows, out_width), bf16),
            pltpu.VMEM((item_rows, width), f32),
            dma(6), dma(2),
        ],
        compiler_params=pltpu.CompilerParams(vmem_limit_bytes=60 * 2**20),
    )(back, total, place, select, item_hidden, item_gain[None, :])


def local(item_hidden, item_gain, history, owner_map, user_gain, value_weight, value_grad):
    chips = lax.axis_size("fsdp") // 2
    moved = 2 * chips * lax.axis_size("dp") * CAP
    by_rows = moved <= value_grad.shape[1] and lax.axis_size("dp") * CAP <= 128
    plan = local_moving_rows if by_rows else local_moving_weight
    return plan(
        item_hidden, item_gain, history, owner_map, user_gain, value_weight, value_grad
    )


def solution(mesh):
    in_specs = (
        P(("dp", "fsdp"), None),
        P(),
        P(("dp", "fsdp")),
        P("fsdp", None),
        P(),
        P("fsdp", None),
        P(("dp", "fsdp"), None),
    )
    out_specs = (P(("dp", "fsdp"), None), P(("dp", "fsdp"), None))
    return jax.shard_map(local, mesh=mesh, in_specs=in_specs, out_specs=out_specs, check_vma=False)
```

```python
import functools
import jax
import jax.numpy as jnp
from jax import lax
from jax.experimental import pallas as pl
from jax.experimental.pallas import tpu as pltpu
from jax.sharding import PartitionSpec as P

CAP = 8
MESH = pl.DeviceIdType.MESH
f32 = jnp.float32
bf16 = jnp.bfloat16


eps = 1e-06


def norm_rows(values, gain):
    scale = lax.rsqrt(jnp.mean(values * values, axis=1, keepdims=True) + eps)
    return (values * scale * gain, scale)


def norm_back(values, gain, scale, upstream):
    unit = values * scale
    scaled = upstream * gain
    return scale * (scaled - unit * jnp.mean(scaled * unit, axis=1, keepdims=True))


def locate(owner_row, items):
    matches = items[:, None] == lax.broadcasted_iota(
        jnp.int32, (items.shape[0], owner_row.shape[0]), 1
    )
    return jnp.sum(jnp.where(matches, owner_row[None, :], 0), axis=1)


def local_moving_weight(item_hidden, item_gain, history, owner_map, user_gain, value_weight, value_grad):
    groups = lax.axis_size("dp")
    here = lax.axis_index("dp")
    item_rows = item_hidden.shape[0]
    hist_rows = history.shape[0]
    width = item_hidden.shape[1]
    owner_row = owner_map[0]
    pool = owner_row.shape[0]
    hidden = item_hidden.astype(jnp.float32)
    item_emb, item_scale = norm_rows(hidden, item_gain)
    item_emb = item_emb.astype(jnp.bfloat16)
    all_history = lax.all_gather(history, "dp", axis=0, tiled=True)
    stored_all = locate(owner_row, all_history).reshape(groups, hist_rows)
    local_rows = lax.broadcasted_iota(jnp.int32, (groups, hist_rows, item_rows), 2)
    wanted = jnp.any(stored_all[:, :, None] == here * item_rows + local_rows, axis=1)
    slot = jnp.cumsum(wanted.astype(jnp.int32), axis=1) - 1
    slot_ids = lax.broadcasted_iota(jnp.int32, (groups, CAP, item_rows), 1)
    select = (wanted[:, None, :] & (slot[:, None, :] == slot_ids)).astype(jnp.bfloat16)
    outgoing = jnp.einsum(
        "dcr,rk->dck", select, item_emb, preferred_element_type=jnp.float32
    ).astype(jnp.bfloat16)
    incoming = lax.all_to_all(outgoing, "dp", split_axis=0, concat_axis=0, tiled=True)
    stored = locate(owner_row, history)
    pick = stored[:, None] == lax.broadcasted_iota(jnp.int32, (hist_rows, pool), 1)
    own_wanted = jnp.any(pick, axis=0).reshape(groups, item_rows)
    own_slot = (jnp.cumsum(own_wanted.astype(jnp.int32), axis=1) - 1).reshape(pool)
    slot_pos = jnp.sum(jnp.where(pick, own_slot[None, :], 0), axis=1)
    buffer_row = stored // item_rows * CAP + slot_pos
    x = jnp.take(incoming.reshape(groups * CAP, width), buffer_row, axis=0).astype(jnp.float32)
    normed, scale = norm_rows(x, user_gain)
    normed = normed.astype(jnp.bfloat16)
    whole = lax.all_gather(value_weight, "fsdp", axis=0, tiled=True)
    values = jnp.dot(normed, whole, preferred_element_type=jnp.float32)
    upstream = lax.dot_general(
        value_grad, whole, (((1,), (1,)), ((), ())), preferred_element_type=jnp.float32
    )
    values = values.astype(jnp.bfloat16)
    dx = norm_back(x, user_gain, scale, upstream)
    one_hot = (
        buffer_row[:, None] == lax.broadcasted_iota(jnp.int32, (hist_rows, groups * CAP), 1)
    ).astype(jnp.float32)
    summed = lax.dot_general(
        one_hot,
        dx,
        (((0,), (0,)), ((), ())),
        precision=lax.Precision.HIGHEST,
        preferred_element_type=jnp.float32,
    )
    returned = lax.all_to_all(
        summed.astype(jnp.bfloat16).reshape(groups, CAP, width),
        "dp",
        split_axis=0,
        concat_axis=0,
        tiled=True,
    )
    emb_grad = jnp.einsum("dcr,dck->rk", select, returned, preferred_element_type=jnp.float32)
    item_grad = norm_back(hidden, item_gain, item_scale, emb_grad)
    return (values, item_grad)


CHUNKS = 2


def iota(shape, dim):
    return lax.broadcasted_iota(jnp.int32, shape, dim)


def dot(a, b, ca=1, cb=0):
    return lax.dot_general(a, b, (((ca,), (cb,)), ((), ())), preferred_element_type=f32)


def fold(rows):
    half = rows.shape[1] // 2
    return jnp.concatenate([rows[:, :half], rows[:, half:]], axis=0)


def unfold(rows):
    return jnp.concatenate([rows[:CAP], rows[CAP:]], axis=1)


def stored_rows(hist, parts, item_rows):
    pool = parts.shape[1]
    named = (iota((pool, hist.shape[1]), 0) == hist).astype(f32).astype(bf16)
    found = dot(parts, named)
    return found[0:1] * item_rows + found[1:2]


def slots(wants, item_rows):
    lane = iota((item_rows, 128), 1)
    wanted = jnp.zeros((item_rows, 128), f32)
    for group, want in enumerate(wants):
        wanted = jnp.where(lane // CAP == group, want, wanted)
    before = (iota((item_rows, item_rows), 1) < iota((item_rows, item_rows), 0)).astype(f32)
    slot = dot(before.astype(bf16), wanted.astype(bf16))
    return jnp.where(slot == (lane % CAP).astype(f32), wanted, 0.0)


def kernel(
    groups, chips,
    item_gain_hbm, history_hbm, owner_hbm, user_gain_hbm, item_hidden, weight, value_grad,
    back_in, total_out, place_out, select_out,
    item_gain, history, owner, user_gain,
    hidden_buf, grad_buf, w_buf, hist_buf, emb_out, emb_in, sum_buf, x_out, x_in,
    part_own, part_out, part_in, up_out, up_in, back_out, total_buf, place_buf, select_buf, wt_buf,
    local_sem, out_sem, w_sem, hello, hist_send, hist_recv, emb_send, emb_recv, sum_send, sum_recv,
    x_send, x_recv, part_send, part_recv, up_send, up_recv, back_send, back_recv,
):
    here = lax.axis_index("dp")
    fsdp = lax.axis_index("fsdp")
    chip = fsdp // 2
    core = fsdp % 2
    item_rows, width = item_hidden.shape
    hist_rows = history.shape[1]
    rows = groups * CAP
    piece = width // chips
    cols = value_grad.shape[1] // CHUNKS
    peers = [lax.rem(here + k, groups) for k in range(1, groups)]
    mates = [lax.rem(chip + k, chips) for k in range(1, chips)]

    def dp_id(peer):
        return (peer, fsdp)

    def chip_id(mate):
        return (here, mate * 2 + core)

    sibling = (here, chip * 2 + 1 - core)

    barrier = pltpu.get_barrier_semaphore()
    group = [dp_id(p) for p in peers] + [chip_id(m) for m in mates]
    for target in group:
        pl.semaphore_signal(barrier, inc=1, device_id=target, device_id_type=MESH)

    loads = [
        pltpu.make_async_copy(src, dst, local_sem.at[k])
        for k, (src, dst) in enumerate([
            (history_hbm, history), (owner_hbm, owner), (value_grad, grad_buf),
            (item_hidden, hidden_buf), (item_gain_hbm, item_gain),
            (user_gain_hbm, user_gain), (weight, w_buf.at[core]),
        ])
    ]
    for load in loads:
        load.start()

    @pl.when(core == 0)
    def _():
        pl.semaphore_wait(barrier, len(group))
        pl.semaphore_signal(barrier, inc=1, device_id=sibling, device_id_type=MESH)

    @pl.when(core == 1)
    def _():
        pl.semaphore_wait(barrier, len(group) + 1)
        pl.semaphore_signal(hello, inc=1, device_id=sibling, device_id_type=MESH)

    w_copy = pltpu.make_async_remote_copy(
        src_ref=weight, dst_ref=w_buf.at[core], send_sem=w_sem.at[0], recv_sem=w_sem.at[1],
        device_id=sibling, device_id_type=MESH,
    )

    @pl.when(core == 1)
    def _():
        w_copy.start()

    def remote(src, dst, send, recv, target):
        return pltpu.make_async_remote_copy(
            src_ref=src, dst_ref=dst, send_sem=send, recv_sem=recv,
            device_id=target, device_id_type=MESH,
        )

    sends = []

    def send_dp(out_of, into, send, recv):
        for k, peer in enumerate(peers):
            copy = remote(out_of(peer), into.at[here], send.at[k], recv.at[here], dp_id(peer))
            copy.start()
            sends.append(copy)

    def wait_dp(into, send, recv):
        for k, peer in enumerate(peers):
            remote(into.at[peer], into.at[peer], send.at[k], recv.at[peer], dp_id(peer)).wait_recv()

    def send_chip(out_of, into, send, recv):
        for k, mate in enumerate(mates):
            copy = remote(out_of(mate), into.at[chip], send.at[k], recv.at[chip], chip_id(mate))
            copy.start()
            sends.append(copy)

    def wait_chip(into, send, recv):
        for k, mate in enumerate(mates):
            remote(into.at[mate], into.at[mate], send.at[k], recv.at[mate], chip_id(mate)).wait_recv()

    send_dp(lambda peer: history_hbm, hist_buf, hist_send, hist_recv)
    loads[0].wait()
    hist_buf[here] = history[...]

    loads[1].wait()
    owner_row = owner[...]
    pool = owner_row.shape[1]
    div = (owner_row // item_rows).astype(f32)
    mod = (owner_row % item_rows).astype(f32)
    parts = jnp.where(iota((8, pool), 0) == 0, div, mod).astype(bf16)

    own = stored_rows(history[...], parts, item_rows)
    match = (iota((pool, hist_rows), 0).astype(f32) == own).astype(f32)
    wants = [
        jnp.max(match[e * item_rows : (e + 1) * item_rows], axis=1, keepdims=True)
        for e in range(groups)
    ]
    one_hot = slots(wants, item_rows)
    lane = iota((item_rows, 128), 1)
    stacked = jnp.concatenate(
        [jnp.where(lane // CAP == e, one_hot, 0.0) for e in range(groups)], axis=0
    )
    place = dot(stacked.astype(bf16), match.astype(bf16), 0, 0)[:rows]
    place = place.astype(bf16)
    place_buf[...] = place
    outs = [pltpu.make_async_copy(place_buf, place_out, out_sem.at[0])]
    outs[0].start()

    loads[2].wait()
    for c in range(CHUNKS):
        sum_buf[c, chip] = dot(place, grad_buf[:, c * cols : (c + 1) * cols]).astype(bf16)
        send_chip(
            lambda mate: sum_buf.at[c, chip], sum_buf.at[c], sum_send.at[c], sum_recv.at[c]
        )

    loads[3].wait()
    loads[4].wait()
    hidden = hidden_buf[...].astype(f32)
    item_scale = lax.rsqrt(jnp.mean(hidden * hidden, axis=1, keepdims=True) + 1e-6)
    item_emb = (hidden * item_scale * item_gain[...]).astype(bf16)

    wait_dp(hist_buf, hist_send, hist_recv)
    base = (here * item_rows).astype(f32)
    local_rows = iota((item_rows, hist_rows), 0).astype(f32) + base
    wants = []
    for t in range(groups):
        stored = stored_rows(hist_buf[t], parts, item_rows)
        wants.append(jnp.max((local_rows == stored).astype(f32), axis=1, keepdims=True))
    select = slots(wants, item_rows)[:, :rows].astype(bf16)
    select_buf[...] = select
    outs.append(pltpu.make_async_copy(select_buf, select_out, out_sem.at[1]))
    outs[1].start()
    outgoing = dot(select, item_emb, 0, 0)
    for t in range(groups):
        emb_out[t] = fold(outgoing[t * CAP : (t + 1) * CAP]).astype(bf16)
    send_dp(lambda peer: emb_out.at[peer], emb_in, emb_send, emb_recv)
    emb_in[here] = emb_out[here]

    @pl.when(core == 0)
    def _():
        pl.semaphore_wait(hello, 1)
        w_copy.start()

    loads[6].wait()
    wt_buf[core] = w_buf[core].T
    loads[5].wait()
    wait_dp(emb_in, emb_send, emb_recv)

    x = jnp.concatenate([unfold(emb_in[e].astype(f32)) for e in range(groups)], axis=0)
    scale = lax.rsqrt(jnp.mean(x * x, axis=1, keepdims=True) + 1e-6)
    normed = (x * scale * user_gain[...]).astype(bf16)
    for p in range(chips):
        x_out[p] = normed[:, p * piece : (p + 1) * piece]
    send_chip(lambda mate: x_out.at[mate], x_in, x_send, x_recv)
    x_in[chip] = x_out[chip]

    w_copy.wait()
    wt_buf[1 - core] = w_buf[1 - core].T
    w_all = w_buf[...].reshape(piece, -1)

    half = piece // 2
    ups = [jnp.zeros((chips * rows, half), f32)] * 2
    for c in range(CHUNKS):
        wait_chip(sum_buf.at[c], sum_send.at[c], sum_recv.at[c])
        sums = sum_buf[c].reshape(chips * rows, cols)
        ups = [ups[h] + dot(sums, wt_buf[h, c * cols : (c + 1) * cols]) for h in range(2)]
    for h in range(2):
        up_out[:, :, h * half : (h + 1) * half] = ups[h].reshape(chips, rows, half)
    send_chip(lambda mate: up_out.at[mate], up_in, up_send, up_recv)
    up_in[chip] = up_out[chip]

    wait_chip(x_in, x_send, x_recv)
    x_all = x_in[...].reshape(chips * rows, piece)
    for c in range(CHUNKS):
        part = dot(x_all, w_all[:, c * cols : (c + 1) * cols]).reshape(chips, rows, cols)
        part_own[c] = part
        part_out[c] = part.astype(bf16)
        send_chip(
            lambda mate: part_out.at[c, mate], part_in.at[c], part_send.at[c], part_recv.at[c]
        )

    wait_chip(up_in, up_send, up_recv)
    upstream = jnp.concatenate([up_in[p] for p in range(chips)], axis=1)
    unit = x * scale
    scaled = upstream * user_gain[...]
    block_sum = scale * (scaled - unit * jnp.mean(scaled * unit, axis=1, keepdims=True))
    for t in range(groups):
        back_out[t] = fold(block_sum[t * CAP : (t + 1) * CAP]).astype(bf16)
    send_dp(lambda peer: back_out.at[peer], back_in, back_send, back_recv)
    outs.append(pltpu.make_async_copy(back_out.at[here], back_in.at[here], out_sem.at[2]))
    outs[2].start()

    for c in range(CHUNKS):
        wait_chip(part_in.at[c], part_send.at[c], part_recv.at[c])
        total = part_own[c, chip]
        for mate in mates:
            total = total + part_in[c, mate].astype(f32)
        total_buf[c] = total.astype(bf16)
        out = pltpu.make_async_copy(total_buf.at[c], total_out.at[c], out_sem.at[3 + c])
        out.start()
        outs.append(out)

    wait_dp(back_in, back_send, back_recv)
    for out in outs:
        out.wait()
    for copy in sends:
        copy.wait_send()


def finish(
    groups, back_hbm, total_hbm, place_hbm, select_hbm, hidden_hbm, gain_hbm,
    values_out, item_grad_out,
    back, total, place, select, hidden_buf, gain, values, item_grad, load_sem, out_sem,
):
    loads = [
        pltpu.make_async_copy(src, dst, load_sem.at[k])
        for k, (src, dst) in enumerate([
            (hidden_hbm, hidden_buf), (gain_hbm, gain), (select_hbm, select), (back_hbm, back),
            (place_hbm, place), (total_hbm, total),
        ])
    ]
    for load in loads:
        load.start()
    loads[0].wait()
    loads[1].wait()
    hidden = hidden_buf[...].astype(f32)
    scale = lax.rsqrt(jnp.mean(hidden * hidden, axis=1, keepdims=True) + 1e-6)
    loads[2].wait()
    loads[3].wait()
    returned = jnp.concatenate([unfold(back[t].astype(f32)) for t in range(groups)], axis=0)
    emb_grad = dot(select[...], returned.astype(bf16))
    unit = hidden * scale
    scaled = emb_grad * gain[...]
    item_grad[...] = scale * (scaled - unit * jnp.mean(scaled * unit, axis=1, keepdims=True))
    grad_copy = pltpu.make_async_copy(item_grad, item_grad_out, out_sem.at[0])
    grad_copy.start()
    loads[4].wait()
    loads[5].wait()
    named = place[...]
    cols = total.shape[2]
    for c in range(CHUNKS):
        values[:, c * cols : (c + 1) * cols] = dot(named, total[c], 0, 0).astype(bf16)
    values_copy = pltpu.make_async_copy(values, values_out, out_sem.at[1])
    values_copy.start()
    grad_copy.wait()
    values_copy.wait()


def local_moving_rows(
    item_hidden, item_gain, history, owner_map, user_gain, value_weight, value_grad
):
    groups = lax.axis_size("dp")
    chips = lax.axis_size("fsdp") // 2
    item_rows, width = item_hidden.shape
    hist_rows, out_width = value_grad.shape
    rows = groups * CAP
    depth = value_weight.shape[0]
    piece = 2 * depth
    cols = out_width // CHUNKS
    hbm = pl.BlockSpec(memory_space=pl.ANY)

    def dma(*counts):
        return pltpu.SemaphoreType.DMA(counts)

    folded = (groups, 2 * CAP, width // 2)
    back, total, place, select = pl.pallas_call(
        functools.partial(kernel, groups, chips),
        out_shape=(
            jax.ShapeDtypeStruct(folded, bf16),
            jax.ShapeDtypeStruct((CHUNKS, rows, cols), bf16),
            jax.ShapeDtypeStruct((rows, hist_rows), bf16),
            jax.ShapeDtypeStruct((item_rows, rows), bf16),
        ),
        in_specs=[hbm] * 7,
        out_specs=(hbm,) * 4,
        scratch_shapes=[
            pltpu.VMEM((1, width), f32),
            pltpu.VMEM((1, hist_rows), jnp.int32),
            pltpu.VMEM((1, owner_map.shape[1]), jnp.int32),
            pltpu.VMEM((1, width), f32),
            pltpu.VMEM((item_rows, width), bf16),
            pltpu.VMEM((hist_rows, out_width), bf16),
            pltpu.VMEM((2, depth, out_width), bf16),
            pltpu.VMEM((groups, 1, hist_rows), jnp.int32),
            pltpu.VMEM(folded, bf16),
            pltpu.VMEM(folded, bf16),
            pltpu.VMEM((CHUNKS, chips, rows, cols), bf16),
            pltpu.VMEM((chips, rows, piece), bf16),
            pltpu.VMEM((chips, rows, piece), bf16),
            pltpu.VMEM((CHUNKS, chips, rows, cols), f32),
            pltpu.VMEM((CHUNKS, chips, rows, cols), bf16),
            pltpu.VMEM((CHUNKS, chips, rows, cols), bf16),
            pltpu.VMEM((chips, rows, piece), f32),
            pltpu.VMEM((chips, rows, piece), f32),
            pltpu.VMEM(folded, bf16),
            pltpu.VMEM((CHUNKS, rows, cols), bf16),
            pltpu.VMEM((rows, hist_rows), bf16),
            pltpu.VMEM((item_rows, rows), bf16),
            pltpu.VMEM((2, out_width, depth), bf16),
            dma(7), dma(3 + CHUNKS), dma(2), pltpu.SemaphoreType.REGULAR,
            dma(groups), dma(groups), dma(groups), dma(groups),
            dma(CHUNKS, chips), dma(CHUNKS, chips), dma(chips), dma(chips),
            dma(CHUNKS, chips), dma(CHUNKS, chips), dma(chips), dma(chips),
            dma(groups), dma(groups),
        ],
        compiler_params=pltpu.CompilerParams(
            collective_id=0, has_side_effects=True, vmem_limit_bytes=60 * 2**20
        ),
    )(
        item_gain[None, :], history[None, :], owner_map, user_gain[None, :],
        item_hidden, value_weight, value_grad,
    )
    return pl.pallas_call(
        functools.partial(finish, groups),
        out_shape=(
            jax.ShapeDtypeStruct((hist_rows, out_width), bf16),
            jax.ShapeDtypeStruct((item_rows, width), f32),
        ),
        in_specs=[hbm] * 6,
        out_specs=(hbm,) * 2,
        scratch_shapes=[
            pltpu.VMEM(folded, bf16),
            pltpu.VMEM((CHUNKS, rows, cols), bf16),
            pltpu.VMEM((rows, hist_rows), bf16),
            pltpu.VMEM((item_rows, rows), bf16),
            pltpu.VMEM((item_rows, width), bf16),
            pltpu.VMEM((1, width), f32),
            pltpu.VMEM((hist_rows, out_width), bf16),
            pltpu.VMEM((item_rows, width), f32),
            dma(6), dma(2),
        ],
        compiler_params=pltpu.CompilerParams(vmem_limit_bytes=60 * 2**20),
    )(back, total, place, select, item_hidden, item_gain[None, :])


def local(item_hidden, item_gain, history, owner_map, user_gain, value_weight, value_grad):
    chips = lax.axis_size("fsdp") // 2
    moved = 2 * chips * lax.axis_size("dp") * CAP
    by_rows = moved <= value_grad.shape[1] and lax.axis_size("dp") * CAP <= 128
    plan = local_moving_rows if by_rows else local_moving_weight
    return plan(
        item_hidden, item_gain, history, owner_map, user_gain, value_weight, value_grad
    )


def solution(mesh):
    in_specs = (
        P(("dp", "fsdp"), None),
        P(),
        P(("dp", "fsdp")),
        P("fsdp", None),
        P(),
        P("fsdp", None),
        P(("dp", "fsdp"), None),
    )
    out_specs = (P(("dp", "fsdp"), None), P(("dp", "fsdp"), None))
    return jax.shard_map(local, mesh=mesh, in_specs=in_specs, out_specs=out_specs, check_vma=False)
```

```python
import functools
import jax
import jax.numpy as jnp
from jax import lax
from jax.experimental import pallas as pl
from jax.experimental.pallas import tpu as pltpu
from jax.sharding import PartitionSpec as P

CAP = 8
MESH = pl.DeviceIdType.MESH
f32 = jnp.float32
bf16 = jnp.bfloat16


eps = 1e-06


def norm_rows(values, gain):
    scale = lax.rsqrt(jnp.mean(values * values, axis=1, keepdims=True) + eps)
    return (values * scale * gain, scale)


def norm_back(values, gain, scale, upstream):
    unit = values * scale
    scaled = upstream * gain
    return scale * (scaled - unit * jnp.mean(scaled * unit, axis=1, keepdims=True))


def locate(owner_row, items):
    matches = items[:, None] == lax.broadcasted_iota(
        jnp.int32, (items.shape[0], owner_row.shape[0]), 1
    )
    return jnp.sum(jnp.where(matches, owner_row[None, :], 0), axis=1)


def local_moving_weight(item_hidden, item_gain, history, owner_map, user_gain, value_weight, value_grad):
    groups = lax.axis_size("dp")
    here = lax.axis_index("dp")
    item_rows = item_hidden.shape[0]
    hist_rows = history.shape[0]
    width = item_hidden.shape[1]
    owner_row = owner_map[0]
    pool = owner_row.shape[0]
    hidden = item_hidden.astype(jnp.float32)
    item_emb, item_scale = norm_rows(hidden, item_gain)
    item_emb = item_emb.astype(jnp.bfloat16)
    all_history = lax.all_gather(history, "dp", axis=0, tiled=True)
    stored_all = locate(owner_row, all_history).reshape(groups, hist_rows)
    local_rows = lax.broadcasted_iota(jnp.int32, (groups, hist_rows, item_rows), 2)
    wanted = jnp.any(stored_all[:, :, None] == here * item_rows + local_rows, axis=1)
    slot = jnp.cumsum(wanted.astype(jnp.int32), axis=1) - 1
    slot_ids = lax.broadcasted_iota(jnp.int32, (groups, CAP, item_rows), 1)
    select = (wanted[:, None, :] & (slot[:, None, :] == slot_ids)).astype(jnp.bfloat16)
    outgoing = jnp.einsum(
        "dcr,rk->dck", select, item_emb, preferred_element_type=jnp.float32
    ).astype(jnp.bfloat16)
    incoming = lax.all_to_all(outgoing, "dp", split_axis=0, concat_axis=0, tiled=True)
    stored = locate(owner_row, history)
    pick = stored[:, None] == lax.broadcasted_iota(jnp.int32, (hist_rows, pool), 1)
    own_wanted = jnp.any(pick, axis=0).reshape(groups, item_rows)
    own_slot = (jnp.cumsum(own_wanted.astype(jnp.int32), axis=1) - 1).reshape(pool)
    slot_pos = jnp.sum(jnp.where(pick, own_slot[None, :], 0), axis=1)
    buffer_row = stored // item_rows * CAP + slot_pos
    x = jnp.take(incoming.reshape(groups * CAP, width), buffer_row, axis=0).astype(jnp.float32)
    normed, scale = norm_rows(x, user_gain)
    normed = normed.astype(jnp.bfloat16)
    whole = lax.all_gather(value_weight, "fsdp", axis=0, tiled=True)
    values = jnp.dot(normed, whole, preferred_element_type=jnp.float32)
    upstream = lax.dot_general(
        value_grad, whole, (((1,), (1,)), ((), ())), preferred_element_type=jnp.float32
    )
    values = values.astype(jnp.bfloat16)
    dx = norm_back(x, user_gain, scale, upstream)
    one_hot = (
        buffer_row[:, None] == lax.broadcasted_iota(jnp.int32, (hist_rows, groups * CAP), 1)
    ).astype(jnp.float32)
    summed = lax.dot_general(
        one_hot,
        dx,
        (((0,), (0,)), ((), ())),
        precision=lax.Precision.HIGHEST,
        preferred_element_type=jnp.float32,
    )
    returned = lax.all_to_all(
        summed.astype(jnp.bfloat16).reshape(groups, CAP, width),
        "dp",
        split_axis=0,
        concat_axis=0,
        tiled=True,
    )
    emb_grad = jnp.einsum("dcr,dck->rk", select, returned, preferred_element_type=jnp.float32)
    item_grad = norm_back(hidden, item_gain, item_scale, emb_grad)
    return (values, item_grad)


CHUNKS = 2
W_COPIES = 8


def iota(shape, dim):
    return lax.broadcasted_iota(jnp.int32, shape, dim)


def dot(a, b, ca=1, cb=0):
    return lax.dot_general(a, b, (((ca,), (cb,)), ((), ())), preferred_element_type=f32)


def fold(rows):
    half = rows.shape[1] // 2
    return jnp.concatenate([rows[:, :half], rows[:, half:]], axis=0)


def unfold(rows):
    return jnp.concatenate([rows[:CAP], rows[CAP:]], axis=1)


def stored_rows(hist, parts, item_rows):
    pool = parts.shape[1]
    named = (iota((pool, hist.shape[1]), 0) == hist).astype(f32).astype(bf16)
    found = dot(parts, named)
    return found[0:1] * item_rows + found[1:2]


def slots(wants, item_rows):
    lane = iota((item_rows, 128), 1)
    wanted = jnp.zeros((item_rows, 128), f32)
    for group, want in enumerate(wants):
        wanted = jnp.where(lane // CAP == group, want, wanted)
    before = (iota((item_rows, item_rows), 1) < iota((item_rows, item_rows), 0)).astype(f32)
    slot = dot(before.astype(bf16), wanted.astype(bf16))
    return jnp.where(slot == (lane % CAP).astype(f32), wanted, 0.0)


def kernel(
    groups, chips,
    item_gain_hbm, history_hbm, owner_hbm, user_gain_hbm, item_hidden, weight, value_grad,
    back_in, total_out, place_out, select_out,
    item_gain, history, owner, user_gain,
    hidden_buf, grad_buf, w_buf, hist_buf, emb_out, emb_in, sum_buf, x_out, x_in,
    part_own, part_out, part_in, up_out, up_in, back_out, total_buf, place_buf, select_buf,
    local_sem, out_sem, w_sem, hello, hist_send, hist_recv, emb_send, emb_recv, sum_send, sum_recv,
    x_send, x_recv, part_send, part_recv, up_send, up_recv, back_send, back_recv,
):
    here = lax.axis_index("dp")
    fsdp = lax.axis_index("fsdp")
    chip = fsdp // 2
    core = fsdp % 2
    item_rows, width = item_hidden.shape
    hist_rows = history.shape[1]
    rows = groups * CAP
    piece = width // chips
    cols = value_grad.shape[1] // CHUNKS
    peers = [lax.rem(here + k, groups) for k in range(1, groups)]
    mates = [lax.rem(chip + k, chips) for k in range(1, chips)]

    def dp_id(peer):
        return (peer, fsdp)

    def chip_id(mate):
        return (here, mate * 2 + core)

    sibling = (here, chip * 2 + 1 - core)

    barrier = pltpu.get_barrier_semaphore()
    group = [dp_id(p) for p in peers] + [chip_id(m) for m in mates]
    for target in group:
        pl.semaphore_signal(barrier, inc=1, device_id=target, device_id_type=MESH)

    loads = [
        pltpu.make_async_copy(src, dst, local_sem.at[k])
        for k, (src, dst) in enumerate([
            (history_hbm, history), (owner_hbm, owner), (value_grad, grad_buf),
            (item_hidden, hidden_buf), (item_gain_hbm, item_gain),
            (user_gain_hbm, user_gain), (weight, w_buf.at[core]),
        ])
    ]
    for load in loads:
        load.start()

    @pl.when(core == 0)
    def _():
        pl.semaphore_wait(barrier, len(group))
        pl.semaphore_signal(barrier, inc=1, device_id=sibling, device_id_type=MESH)

    @pl.when(core == 1)
    def _():
        pl.semaphore_wait(barrier, len(group) + 1)
        pl.semaphore_signal(hello, inc=1, device_id=sibling, device_id_type=MESH)

    stripe = weight.shape[0] // W_COPIES
    w_copies = [
        pltpu.make_async_remote_copy(
            src_ref=weight.at[pl.ds(k * stripe, stripe)],
            dst_ref=w_buf.at[core, pl.ds(k * stripe, stripe)],
            send_sem=w_sem.at[0, k], recv_sem=w_sem.at[1, k],
            device_id=sibling, device_id_type=MESH,
        )
        for k in range(W_COPIES)
    ]

    @pl.when(core == 1)
    def _():
        for copy in w_copies:
            copy.start()

    def remote(src, dst, send, recv, target):
        return pltpu.make_async_remote_copy(
            src_ref=src, dst_ref=dst, send_sem=send, recv_sem=recv,
            device_id=target, device_id_type=MESH,
        )

    sends = []

    def send_dp(out_of, into, send, recv):
        for k, peer in enumerate(peers):
            copy = remote(out_of(peer), into.at[here], send.at[k], recv.at[here], dp_id(peer))
            copy.start()
            sends.append(copy)

    def wait_dp(into, send, recv):
        for k, peer in enumerate(peers):
            remote(into.at[peer], into.at[peer], send.at[k], recv.at[peer], dp_id(peer)).wait_recv()

    def send_chip(out_of, into, send, recv):
        for k, mate in enumerate(mates):
            copy = remote(out_of(mate), into.at[chip], send.at[k], recv.at[chip], chip_id(mate))
            copy.start()
            sends.append(copy)

    def wait_chip(into, send, recv):
        for k, mate in enumerate(mates):
            remote(into.at[mate], into.at[mate], send.at[k], recv.at[mate], chip_id(mate)).wait_recv()

    send_dp(lambda peer: history_hbm, hist_buf, hist_send, hist_recv)
    loads[0].wait()
    hist_buf[here] = history[...]

    loads[1].wait()
    owner_row = owner[...]
    pool = owner_row.shape[1]
    div = (owner_row // item_rows).astype(f32)
    mod = (owner_row % item_rows).astype(f32)
    parts = jnp.where(iota((8, pool), 0) == 0, div, mod).astype(bf16)

    own = stored_rows(history[...], parts, item_rows)
    match = (iota((pool, hist_rows), 0).astype(f32) == own).astype(f32)
    wants = [
        jnp.max(match[e * item_rows : (e + 1) * item_rows], axis=1, keepdims=True)
        for e in range(groups)
    ]
    one_hot = slots(wants, item_rows)
    lane = iota((item_rows, 128), 1)
    stacked = jnp.concatenate(
        [jnp.where(lane // CAP == e, one_hot, 0.0) for e in range(groups)], axis=0
    )
    place = dot(stacked.astype(bf16), match.astype(bf16), 0, 0)[:rows]
    place = place.astype(bf16)
    place_buf[...] = place
    outs = [pltpu.make_async_copy(place_buf, place_out, out_sem.at[0])]
    outs[0].start()

    loads[2].wait()
    for c in range(CHUNKS):
        sum_buf[c, chip] = dot(place, grad_buf[:, c * cols : (c + 1) * cols]).astype(bf16)
        send_chip(
            lambda mate: sum_buf.at[c, chip], sum_buf.at[c], sum_send.at[c], sum_recv.at[c]
        )

    loads[3].wait()
    loads[4].wait()
    hidden = hidden_buf[...].astype(f32)
    item_scale = lax.rsqrt(jnp.mean(hidden * hidden, axis=1, keepdims=True) + 1e-6)
    item_emb = (hidden * item_scale * item_gain[...]).astype(bf16)

    @pl.when(core == 0)
    def _():
        pl.semaphore_wait(hello, 1)
        for copy in w_copies:
            copy.start()

    wait_dp(hist_buf, hist_send, hist_recv)
    base = (here * item_rows).astype(f32)
    local_rows = iota((item_rows, hist_rows), 0).astype(f32) + base
    wants = []
    for t in range(groups):
        stored = stored_rows(hist_buf[t], parts, item_rows)
        wants.append(jnp.max((local_rows == stored).astype(f32), axis=1, keepdims=True))
    select = slots(wants, item_rows)[:, :rows].astype(bf16)
    select_buf[...] = select
    outs.append(pltpu.make_async_copy(select_buf, select_out, out_sem.at[1]))
    outs[1].start()
    outgoing = dot(select, item_emb, 0, 0)
    for t in range(groups):
        emb_out[t] = fold(outgoing[t * CAP : (t + 1) * CAP]).astype(bf16)
    send_dp(lambda peer: emb_out.at[peer], emb_in, emb_send, emb_recv)
    emb_in[here] = emb_out[here]

    loads[5].wait()
    wait_dp(emb_in, emb_send, emb_recv)

    x = jnp.concatenate([unfold(emb_in[e].astype(f32)) for e in range(groups)], axis=0)
    scale = lax.rsqrt(jnp.mean(x * x, axis=1, keepdims=True) + 1e-6)
    normed = (x * scale * user_gain[...]).astype(bf16)
    for p in range(chips):
        x_out[p] = normed[:, p * piece : (p + 1) * piece]
    send_chip(lambda mate: x_out.at[mate], x_in, x_send, x_recv)
    x_in[chip] = x_out[chip]

    depth = weight.shape[0]

    def half_columns(half):
        return pl.ds(pl.multiple_of(half * depth, depth), depth)

    def up_half(half):
        up = jnp.zeros((chips * rows, depth), f32)
        for c in range(CHUNKS):
            sums = sum_buf[c].reshape(chips * rows, cols)
            up = up + dot(sums, w_buf[half, :, c * cols : (c + 1) * cols], 1, 1)
        up_out[:, :, half_columns(half)] = up.reshape(chips, rows, depth)

    def part_half(half, c):
        x_half = x_in[:, :, half_columns(half)].reshape(chips * rows, depth)
        part = dot(x_half, w_buf[half, :, c * cols : (c + 1) * cols])
        return part.reshape(chips, rows, cols)

    loads[6].wait()
    for c in range(CHUNKS):
        wait_chip(sum_buf.at[c], sum_send.at[c], sum_recv.at[c])
    up_half(core)
    wait_chip(x_in, x_send, x_recv)
    for c in range(CHUNKS):
        part_own[c] = part_half(core, c)

    for copy in w_copies:
        copy.wait()
    up_half(1 - core)
    send_chip(lambda mate: up_out.at[mate], up_in, up_send, up_recv)
    up_in[chip] = up_out[chip]
    for c in range(CHUNKS):
        part = part_own[c] + part_half(1 - core, c)
        part_own[c] = part
        part_out[c] = part.astype(bf16)
        send_chip(
            lambda mate: part_out.at[c, mate], part_in.at[c], part_send.at[c], part_recv.at[c]
        )

    wait_chip(up_in, up_send, up_recv)
    upstream = jnp.concatenate([up_in[p] for p in range(chips)], axis=1)
    unit = x * scale
    scaled = upstream * user_gain[...]
    block_sum = scale * (scaled - unit * jnp.mean(scaled * unit, axis=1, keepdims=True))
    for t in range(groups):
        back_out[t] = fold(block_sum[t * CAP : (t + 1) * CAP]).astype(bf16)
    send_dp(lambda peer: back_out.at[peer], back_in, back_send, back_recv)
    outs.append(pltpu.make_async_copy(back_out.at[here], back_in.at[here], out_sem.at[2]))
    outs[2].start()

    for c in range(CHUNKS):
        wait_chip(part_in.at[c], part_send.at[c], part_recv.at[c])
        total = part_own[c, chip]
        for mate in mates:
            total = total + part_in[c, mate].astype(f32)
        total_buf[c] = total.astype(bf16)
        out = pltpu.make_async_copy(total_buf.at[c], total_out.at[c], out_sem.at[3 + c])
        out.start()
        outs.append(out)

    wait_dp(back_in, back_send, back_recv)
    for out in outs:
        out.wait()
    for copy in sends:
        copy.wait_send()


def finish(
    groups, back_hbm, total_hbm, place_hbm, select_hbm, hidden_hbm, gain_hbm,
    values_out, item_grad_out,
    back, total, place, select, hidden_buf, gain, values, item_grad, load_sem, out_sem,
):
    loads = [
        pltpu.make_async_copy(src, dst, load_sem.at[k])
        for k, (src, dst) in enumerate([
            (hidden_hbm, hidden_buf), (gain_hbm, gain), (select_hbm, select), (back_hbm, back),
            (place_hbm, place), (total_hbm, total),
        ])
    ]
    for load in loads:
        load.start()
    loads[0].wait()
    loads[1].wait()
    hidden = hidden_buf[...].astype(f32)
    scale = lax.rsqrt(jnp.mean(hidden * hidden, axis=1, keepdims=True) + 1e-6)
    loads[2].wait()
    loads[3].wait()
    returned = jnp.concatenate([unfold(back[t].astype(f32)) for t in range(groups)], axis=0)
    emb_grad = dot(select[...], returned.astype(bf16))
    unit = hidden * scale
    scaled = emb_grad * gain[...]
    item_grad[...] = scale * (scaled - unit * jnp.mean(scaled * unit, axis=1, keepdims=True))
    grad_copy = pltpu.make_async_copy(item_grad, item_grad_out, out_sem.at[0])
    grad_copy.start()
    loads[4].wait()
    loads[5].wait()
    named = place[...]
    cols = total.shape[2]
    for c in range(CHUNKS):
        values[:, c * cols : (c + 1) * cols] = dot(named, total[c], 0, 0).astype(bf16)
    values_copy = pltpu.make_async_copy(values, values_out, out_sem.at[1])
    values_copy.start()
    grad_copy.wait()
    values_copy.wait()


def local_moving_rows(
    item_hidden, item_gain, history, owner_map, user_gain, value_weight, value_grad
):
    groups = lax.axis_size("dp")
    chips = lax.axis_size("fsdp") // 2
    item_rows, width = item_hidden.shape
    hist_rows, out_width = value_grad.shape
    rows = groups * CAP
    depth = value_weight.shape[0]
    piece = 2 * depth
    cols = out_width // CHUNKS
    hbm = pl.BlockSpec(memory_space=pl.ANY)

    def dma(*counts):
        return pltpu.SemaphoreType.DMA(counts)

    folded = (groups, 2 * CAP, width // 2)
    back, total, place, select = pl.pallas_call(
        functools.partial(kernel, groups, chips),
        out_shape=(
            jax.ShapeDtypeStruct(folded, bf16),
            jax.ShapeDtypeStruct((CHUNKS, rows, cols), bf16),
            jax.ShapeDtypeStruct((rows, hist_rows), bf16),
            jax.ShapeDtypeStruct((item_rows, rows), bf16),
        ),
        in_specs=[hbm] * 7,
        out_specs=(hbm,) * 4,
        scratch_shapes=[
            pltpu.VMEM((1, width), f32),
            pltpu.VMEM((1, hist_rows), jnp.int32),
            pltpu.VMEM((1, owner_map.shape[1]), jnp.int32),
            pltpu.VMEM((1, width), f32),
            pltpu.VMEM((item_rows, width), bf16),
            pltpu.VMEM((hist_rows, out_width), bf16),
            pltpu.VMEM((2, depth, out_width), bf16),
            pltpu.VMEM((groups, 1, hist_rows), jnp.int32),
            pltpu.VMEM(folded, bf16),
            pltpu.VMEM(folded, bf16),
            pltpu.VMEM((CHUNKS, chips, rows, cols), bf16),
            pltpu.VMEM((chips, rows, piece), bf16),
            pltpu.VMEM((chips, rows, piece), bf16),
            pltpu.VMEM((CHUNKS, chips, rows, cols), f32),
            pltpu.VMEM((CHUNKS, chips, rows, cols), bf16),
            pltpu.VMEM((CHUNKS, chips, rows, cols), bf16),
            pltpu.VMEM((chips, rows, piece), f32),
            pltpu.VMEM((chips, rows, piece), f32),
            pltpu.VMEM(folded, bf16),
            pltpu.VMEM((CHUNKS, rows, cols), bf16),
            pltpu.VMEM((rows, hist_rows), bf16),
            pltpu.VMEM((item_rows, rows), bf16),
            dma(7), dma(3 + CHUNKS), dma(2, W_COPIES), pltpu.SemaphoreType.REGULAR,
            dma(groups), dma(groups), dma(groups), dma(groups),
            dma(CHUNKS, chips), dma(CHUNKS, chips), dma(chips), dma(chips),
            dma(CHUNKS, chips), dma(CHUNKS, chips), dma(chips), dma(chips),
            dma(groups), dma(groups),
        ],
        compiler_params=pltpu.CompilerParams(
            collective_id=0, has_side_effects=True, vmem_limit_bytes=60 * 2**20
        ),
    )(
        item_gain[None, :], history[None, :], owner_map, user_gain[None, :],
        item_hidden, value_weight, value_grad,
    )
    return pl.pallas_call(
        functools.partial(finish, groups),
        out_shape=(
            jax.ShapeDtypeStruct((hist_rows, out_width), bf16),
            jax.ShapeDtypeStruct((item_rows, width), f32),
        ),
        in_specs=[hbm] * 6,
        out_specs=(hbm,) * 2,
        scratch_shapes=[
            pltpu.VMEM(folded, bf16),
            pltpu.VMEM((CHUNKS, rows, cols), bf16),
            pltpu.VMEM((rows, hist_rows), bf16),
            pltpu.VMEM((item_rows, rows), bf16),
            pltpu.VMEM((item_rows, width), bf16),
            pltpu.VMEM((1, width), f32),
            pltpu.VMEM((hist_rows, out_width), bf16),
            pltpu.VMEM((item_rows, width), f32),
            dma(6), dma(2),
        ],
        compiler_params=pltpu.CompilerParams(vmem_limit_bytes=60 * 2**20),
    )(back, total, place, select, item_hidden, item_gain[None, :])


def local(item_hidden, item_gain, history, owner_map, user_gain, value_weight, value_grad):
    chips = lax.axis_size("fsdp") // 2
    moved = 2 * chips * lax.axis_size("dp") * CAP
    by_rows = moved <= value_grad.shape[1] and lax.axis_size("dp") * CAP <= 128
    plan = local_moving_rows if by_rows else local_moving_weight
    return plan(
        item_hidden, item_gain, history, owner_map, user_gain, value_weight, value_grad
    )


def solution(mesh):
    in_specs = (
        P(("dp", "fsdp"), None),
        P(),
        P(("dp", "fsdp")),
        P("fsdp", None),
        P(),
        P("fsdp", None),
        P(("dp", "fsdp"), None),
    )
    out_specs = (P(("dp", "fsdp"), None), P(("dp", "fsdp"), None))
    return jax.shard_map(local, mesh=mesh, in_specs=in_specs, out_specs=out_specs, check_vma=False)
```

```python
import functools
import jax
import jax.numpy as jnp
from jax import lax
from jax.experimental import pallas as pl
from jax.experimental.pallas import tpu as pltpu
from jax.sharding import PartitionSpec as P

CAP = 8
MESH = pl.DeviceIdType.MESH
f32 = jnp.float32
bf16 = jnp.bfloat16


eps = 1e-06


def norm_rows(values, gain):
    scale = lax.rsqrt(jnp.mean(values * values, axis=1, keepdims=True) + eps)
    return (values * scale * gain, scale)


def norm_back(values, gain, scale, upstream):
    unit = values * scale
    scaled = upstream * gain
    return scale * (scaled - unit * jnp.mean(scaled * unit, axis=1, keepdims=True))


def locate(owner_row, items):
    matches = items[:, None] == lax.broadcasted_iota(
        jnp.int32, (items.shape[0], owner_row.shape[0]), 1
    )
    return jnp.sum(jnp.where(matches, owner_row[None, :], 0), axis=1)


def local_moving_weight(item_hidden, item_gain, history, owner_map, user_gain, value_weight, value_grad):
    groups = lax.axis_size("dp")
    here = lax.axis_index("dp")
    item_rows = item_hidden.shape[0]
    hist_rows = history.shape[0]
    width = item_hidden.shape[1]
    owner_row = owner_map[0]
    pool = owner_row.shape[0]
    hidden = item_hidden.astype(jnp.float32)
    item_emb, item_scale = norm_rows(hidden, item_gain)
    item_emb = item_emb.astype(jnp.bfloat16)
    all_history = lax.all_gather(history, "dp", axis=0, tiled=True)
    stored_all = locate(owner_row, all_history).reshape(groups, hist_rows)
    local_rows = lax.broadcasted_iota(jnp.int32, (groups, hist_rows, item_rows), 2)
    wanted = jnp.any(stored_all[:, :, None] == here * item_rows + local_rows, axis=1)
    slot = jnp.cumsum(wanted.astype(jnp.int32), axis=1) - 1
    slot_ids = lax.broadcasted_iota(jnp.int32, (groups, CAP, item_rows), 1)
    select = (wanted[:, None, :] & (slot[:, None, :] == slot_ids)).astype(jnp.bfloat16)
    outgoing = jnp.einsum(
        "dcr,rk->dck", select, item_emb, preferred_element_type=jnp.float32
    ).astype(jnp.bfloat16)
    incoming = lax.all_to_all(outgoing, "dp", split_axis=0, concat_axis=0, tiled=True)
    stored = locate(owner_row, history)
    pick = stored[:, None] == lax.broadcasted_iota(jnp.int32, (hist_rows, pool), 1)
    own_wanted = jnp.any(pick, axis=0).reshape(groups, item_rows)
    own_slot = (jnp.cumsum(own_wanted.astype(jnp.int32), axis=1) - 1).reshape(pool)
    slot_pos = jnp.sum(jnp.where(pick, own_slot[None, :], 0), axis=1)
    buffer_row = stored // item_rows * CAP + slot_pos
    x = jnp.take(incoming.reshape(groups * CAP, width), buffer_row, axis=0).astype(jnp.float32)
    normed, scale = norm_rows(x, user_gain)
    normed = normed.astype(jnp.bfloat16)
    whole = lax.all_gather(value_weight, "fsdp", axis=0, tiled=True)
    values = jnp.dot(normed, whole, preferred_element_type=jnp.float32)
    upstream = lax.dot_general(
        value_grad, whole, (((1,), (1,)), ((), ())), preferred_element_type=jnp.float32
    )
    values = values.astype(jnp.bfloat16)
    dx = norm_back(x, user_gain, scale, upstream)
    one_hot = (
        buffer_row[:, None] == lax.broadcasted_iota(jnp.int32, (hist_rows, groups * CAP), 1)
    ).astype(jnp.float32)
    summed = lax.dot_general(
        one_hot,
        dx,
        (((0,), (0,)), ((), ())),
        precision=lax.Precision.HIGHEST,
        preferred_element_type=jnp.float32,
    )
    returned = lax.all_to_all(
        summed.astype(jnp.bfloat16).reshape(groups, CAP, width),
        "dp",
        split_axis=0,
        concat_axis=0,
        tiled=True,
    )
    emb_grad = jnp.einsum("dcr,dck->rk", select, returned, preferred_element_type=jnp.float32)
    item_grad = norm_back(hidden, item_gain, item_scale, emb_grad)
    return (values, item_grad)


CHUNKS = 4


def iota(shape, dim):
    return lax.broadcasted_iota(jnp.int32, shape, dim)


def dot(a, b, ca=1, cb=0):
    return lax.dot_general(a, b, (((ca,), (cb,)), ((), ())), preferred_element_type=f32)


def fold(rows):
    half = rows.shape[1] // 2
    return jnp.concatenate([rows[:, :half], rows[:, half:]], axis=0)


def unfold(rows):
    return jnp.concatenate([rows[:CAP], rows[CAP:]], axis=1)


def stored_rows(hist, parts, item_rows):
    pool = parts.shape[1]
    named = (iota((pool, hist.shape[1]), 0) == hist).astype(f32).astype(bf16)
    found = dot(parts, named)
    return found[0:1] * item_rows + found[1:2]


def slots(wants, item_rows):
    lane = iota((item_rows, 128), 1)
    wanted = jnp.zeros((item_rows, 128), f32)
    for group, want in enumerate(wants):
        wanted = jnp.where(lane // CAP == group, want, wanted)
    before = (iota((item_rows, item_rows), 1) < iota((item_rows, item_rows), 0)).astype(f32)
    slot = dot(before.astype(bf16), wanted.astype(bf16))
    return jnp.where(slot == (lane % CAP).astype(f32), wanted, 0.0)


def kernel(
    groups, chips,
    item_gain_hbm, history_hbm, owner_hbm, user_gain_hbm, item_hidden, weight, value_grad,
    back_in, total_in, place_out, select_out,
    item_gain, history, owner, user_gain,
    hidden_buf, grad_buf, w_buf, hist_buf, emb_out, emb_in, sum_buf, x_out, x_in,
    part_own, part_out, part_in, up_out, up_in, back_out, total_buf, place_buf, select_buf,
    local_sem, out_sem, w_sem, hello, hist_send, hist_recv, emb_send, emb_recv, sum_send, sum_recv,
    x_send, x_recv, part_send, part_recv, up_send, up_recv, back_send, back_recv, total_send, total_recv,
):
    here = lax.axis_index("dp")
    fsdp = lax.axis_index("fsdp")
    chip = fsdp // 2
    core = fsdp % 2
    item_rows, width = item_hidden.shape
    hist_rows = history.shape[1]
    rows = groups * CAP
    piece = width // chips
    cols = value_grad.shape[1] // CHUNKS
    peers = [lax.rem(here + k, groups) for k in range(1, groups)]
    mates = [lax.rem(chip + k, chips) for k in range(1, chips)]

    def dp_id(peer):
        return (peer, fsdp)

    def chip_id(mate):
        return (here, mate * 2 + core)

    sibling = (here, chip * 2 + 1 - core)

    barrier = pltpu.get_barrier_semaphore()
    group = [dp_id(p) for p in peers] + [chip_id(m) for m in mates]
    for target in group:
        pl.semaphore_signal(barrier, inc=1, device_id=target, device_id_type=MESH)

    loads = [
        pltpu.make_async_copy(src, dst, local_sem.at[k])
        for k, (src, dst) in enumerate([
            (history_hbm, history), (owner_hbm, owner), (value_grad, grad_buf),
            (item_hidden, hidden_buf), (item_gain_hbm, item_gain),
            (user_gain_hbm, user_gain), (weight, w_buf.at[core]),
        ])
    ]
    for load in loads:
        load.start()

    @pl.when(core == 0)
    def _():
        pl.semaphore_wait(barrier, len(group))
        pl.semaphore_signal(barrier, inc=1, device_id=sibling, device_id_type=MESH)

    @pl.when(core == 1)
    def _():
        pl.semaphore_wait(barrier, len(group) + 1)
        pl.semaphore_signal(hello, inc=1, device_id=sibling, device_id_type=MESH)

    w_copy = pltpu.make_async_remote_copy(
        src_ref=weight, dst_ref=w_buf.at[core], send_sem=w_sem.at[0], recv_sem=w_sem.at[1],
        device_id=sibling, device_id_type=MESH,
    )

    @pl.when(core == 1)
    def _():
        w_copy.start()

    def remote(src, dst, send, recv, target):
        return pltpu.make_async_remote_copy(
            src_ref=src, dst_ref=dst, send_sem=send, recv_sem=recv,
            device_id=target, device_id_type=MESH,
        )

    sends = []

    def send_dp(out_of, into, send, recv):
        for k, peer in enumerate(peers):
            copy = remote(out_of(peer), into.at[here], send.at[k], recv.at[here], dp_id(peer))
            copy.start()
            sends.append(copy)

    def wait_dp(into, send, recv):
        for k, peer in enumerate(peers):
            remote(into.at[peer], into.at[peer], send.at[k], recv.at[peer], dp_id(peer)).wait_recv()

    def send_chip(out_of, into, send, recv):
        for k, mate in enumerate(mates):
            copy = remote(out_of(mate), into.at[chip], send.at[k], recv.at[chip], chip_id(mate))
            copy.start()
            sends.append(copy)

    def wait_chip(into, send, recv):
        for k, mate in enumerate(mates):
            remote(into.at[mate], into.at[mate], send.at[k], recv.at[mate], chip_id(mate)).wait_recv()

    send_dp(lambda peer: history_hbm, hist_buf, hist_send, hist_recv)
    loads[0].wait()
    hist_buf[here] = history[...]

    loads[1].wait()
    owner_row = owner[...]
    pool = owner_row.shape[1]
    div = (owner_row // item_rows).astype(f32)
    mod = (owner_row % item_rows).astype(f32)
    parts = jnp.where(iota((8, pool), 0) == 0, div, mod).astype(bf16)

    own = stored_rows(history[...], parts, item_rows)
    match = (iota((pool, hist_rows), 0).astype(f32) == own).astype(f32)
    wants = [
        jnp.max(match[e * item_rows : (e + 1) * item_rows], axis=1, keepdims=True)
        for e in range(groups)
    ]
    one_hot = slots(wants, item_rows)
    lane = iota((item_rows, 128), 1)
    stacked = jnp.concatenate(
        [jnp.where(lane // CAP == e, one_hot, 0.0) for e in range(groups)], axis=0
    )
    place = dot(stacked.astype(bf16), match.astype(bf16), 0, 0)[:rows]
    place = place.astype(bf16)
    place_buf[...] = place
    outs = [pltpu.make_async_copy(place_buf, place_out, out_sem.at[0])]
    outs[0].start()

    loads[2].wait()
    for c in range(CHUNKS):
        sum_buf[c, chip] = dot(place, grad_buf[:, c * cols : (c + 1) * cols]).astype(bf16)
        send_chip(
            lambda mate: sum_buf.at[c, chip], sum_buf.at[c], sum_send.at[c], sum_recv.at[c]
        )

    loads[3].wait()
    loads[4].wait()
    hidden = hidden_buf[...].astype(f32)
    item_scale = lax.rsqrt(jnp.mean(hidden * hidden, axis=1, keepdims=True) + 1e-6)
    item_emb = (hidden * item_scale * item_gain[...]).astype(bf16)
    loads[5].wait()
    held = item_emb.astype(f32)
    held_scale = lax.rsqrt(jnp.mean(held * held, axis=1, keepdims=True) + 1e-6)
    held_normed = (held * held_scale * user_gain[...]).astype(bf16)

    wait_dp(hist_buf, hist_send, hist_recv)
    base = (here * item_rows).astype(f32)
    local_rows = iota((item_rows, hist_rows), 0).astype(f32) + base
    wants = []
    for t in range(groups):
        stored = stored_rows(hist_buf[t], parts, item_rows)
        wants.append(jnp.max((local_rows == stored).astype(f32), axis=1, keepdims=True))
    select = slots(wants, item_rows)[:, :rows].astype(bf16)
    select_buf[...] = select
    outs.append(pltpu.make_async_copy(select_buf, select_out, out_sem.at[1]))
    outs[1].start()
    normed = dot(select, held_normed, 0, 0).astype(bf16)
    for p in range(chips):
        x_out[p] = normed[:, p * piece : (p + 1) * piece]
    send_chip(lambda mate: x_out.at[mate], x_in, x_send, x_recv)
    x_in[chip] = x_out[chip]
    outgoing = dot(select, item_emb, 0, 0)
    for t in range(groups):
        emb_out[t] = fold(outgoing[t * CAP : (t + 1) * CAP]).astype(bf16)
    send_dp(lambda peer: emb_out.at[peer], emb_in, emb_send, emb_recv)
    emb_in[here] = emb_out[here]

    @pl.when(core == 0)
    def _():
        pl.semaphore_wait(hello, 1)
        w_copy.start()

    loads[6].wait()
    w_copy.wait()
    w_all = w_buf[...].reshape(piece, -1)

    up = jnp.zeros((chips * rows, piece), f32)
    for c in range(CHUNKS):
        wait_chip(sum_buf.at[c], sum_send.at[c], sum_recv.at[c])
        sums = sum_buf[c].reshape(chips * rows, cols)
        up = up + dot(sums, w_all[:, c * cols : (c + 1) * cols], 1, 1)
    up_out[...] = up.reshape(chips, rows, piece)
    send_chip(lambda mate: up_out.at[mate], up_in, up_send, up_recv)
    up_in[chip] = up_out[chip]

    wait_chip(x_in, x_send, x_recv)
    x_all = x_in[...].reshape(chips * rows, piece)
    for c in range(CHUNKS):
        part = dot(x_all, w_all[:, c * cols : (c + 1) * cols]).reshape(chips, rows, cols)
        part_own[c] = part
        part_out[c] = part.astype(bf16)
        send_chip(
            lambda mate: part_out.at[c, mate], part_in.at[c], part_send.at[c], part_recv.at[c]
        )

    wait_dp(emb_in, emb_send, emb_recv)
    x = jnp.concatenate([unfold(emb_in[e].astype(f32)) for e in range(groups)], axis=0)
    scale = lax.rsqrt(jnp.mean(x * x, axis=1, keepdims=True) + 1e-6)
    wait_chip(up_in, up_send, up_recv)
    upstream = jnp.concatenate([up_in[p] for p in range(chips)], axis=1)
    unit = x * scale
    scaled = upstream * user_gain[...]
    block_sum = scale * (scaled - unit * jnp.mean(scaled * unit, axis=1, keepdims=True))
    for t in range(groups):
        back_out[t] = fold(block_sum[t * CAP : (t + 1) * CAP]).astype(bf16)
    send_dp(lambda peer: back_out.at[peer], back_in, back_send, back_recv)
    outs.append(pltpu.make_async_copy(back_out.at[here], back_in.at[here], out_sem.at[2]))
    outs[2].start()

    for c in range(CHUNKS):
        wait_chip(part_in.at[c], part_send.at[c], part_recv.at[c])
        total = part_own[c, chip]
        for mate in mates:
            total = total + part_in[c, mate].astype(f32)
        for t in range(groups):
            total_buf[c, t] = fold(total[t * CAP : (t + 1) * CAP]).astype(bf16)
        send_dp(
            lambda peer: total_buf.at[c, peer], total_in.at[c], total_send.at[c], total_recv.at[c]
        )
        out = pltpu.make_async_copy(
            total_buf.at[c, here], total_in.at[c, here], out_sem.at[3 + c]
        )
        out.start()
        outs.append(out)

    wait_dp(back_in, back_send, back_recv)
    for c in range(CHUNKS):
        wait_dp(total_in.at[c], total_send.at[c], total_recv.at[c])
    for out in outs:
        out.wait()
    for copy in sends:
        copy.wait_send()


def finish(
    groups, back_hbm, total_hbm, place_hbm, select_hbm, hidden_hbm, gain_hbm,
    values_out, item_grad_out,
    back, total, place, select, hidden_buf, gain, values, item_grad, load_sem, out_sem,
):
    loads = [
        pltpu.make_async_copy(src, dst, load_sem.at[k])
        for k, (src, dst) in enumerate([
            (hidden_hbm, hidden_buf), (gain_hbm, gain), (select_hbm, select), (back_hbm, back),
            (place_hbm, place), (total_hbm, total),
        ])
    ]
    for load in loads:
        load.start()
    loads[0].wait()
    loads[1].wait()
    hidden = hidden_buf[...].astype(f32)
    scale = lax.rsqrt(jnp.mean(hidden * hidden, axis=1, keepdims=True) + 1e-6)
    loads[2].wait()
    loads[3].wait()
    returned = jnp.concatenate([unfold(back[t].astype(f32)) for t in range(groups)], axis=0)
    emb_grad = dot(select[...], returned.astype(bf16))
    unit = hidden * scale
    scaled = emb_grad * gain[...]
    item_grad[...] = scale * (scaled - unit * jnp.mean(scaled * unit, axis=1, keepdims=True))
    grad_copy = pltpu.make_async_copy(item_grad, item_grad_out, out_sem.at[0])
    grad_copy.start()
    loads[4].wait()
    loads[5].wait()
    named = place[...]
    cols = values.shape[1] // CHUNKS
    for c in range(CHUNKS):
        rows = [unfold(total[c, e].astype(f32)) for e in range(groups)]
        rows = jnp.concatenate(rows, axis=0).astype(bf16)
        values[:, c * cols : (c + 1) * cols] = dot(named, rows, 0, 0).astype(bf16)
    values_copy = pltpu.make_async_copy(values, values_out, out_sem.at[1])
    values_copy.start()
    grad_copy.wait()
    values_copy.wait()


def local_moving_rows(
    item_hidden, item_gain, history, owner_map, user_gain, value_weight, value_grad
):
    groups = lax.axis_size("dp")
    chips = lax.axis_size("fsdp") // 2
    item_rows, width = item_hidden.shape
    hist_rows, out_width = value_grad.shape
    rows = groups * CAP
    depth = value_weight.shape[0]
    piece = 2 * depth
    cols = out_width // CHUNKS
    hbm = pl.BlockSpec(memory_space=pl.ANY)

    def dma(*counts):
        return pltpu.SemaphoreType.DMA(counts)

    folded = (groups, 2 * CAP, width // 2)
    back, total, place, select = pl.pallas_call(
        functools.partial(kernel, groups, chips),
        out_shape=(
            jax.ShapeDtypeStruct(folded, bf16),
            jax.ShapeDtypeStruct((CHUNKS, groups, 2 * CAP, cols // 2), bf16),
            jax.ShapeDtypeStruct((rows, hist_rows), bf16),
            jax.ShapeDtypeStruct((item_rows, rows), bf16),
        ),
        in_specs=[hbm] * 7,
        out_specs=(hbm,) * 4,
        scratch_shapes=[
            pltpu.VMEM((1, width), f32),
            pltpu.VMEM((1, hist_rows), jnp.int32),
            pltpu.VMEM((1, owner_map.shape[1]), jnp.int32),
            pltpu.VMEM((1, width), f32),
            pltpu.VMEM((item_rows, width), bf16),
            pltpu.VMEM((hist_rows, out_width), bf16),
            pltpu.VMEM((2, depth, out_width), bf16),
            pltpu.VMEM((groups, 1, hist_rows), jnp.int32),
            pltpu.VMEM(folded, bf16),
            pltpu.VMEM(folded, bf16),
            pltpu.VMEM((CHUNKS, chips, rows, cols), bf16),
            pltpu.VMEM((chips, rows, piece), bf16),
            pltpu.VMEM((chips, rows, piece), bf16),
            pltpu.VMEM((CHUNKS, chips, rows, cols), f32),
            pltpu.VMEM((CHUNKS, chips, rows, cols), bf16),
            pltpu.VMEM((CHUNKS, chips, rows, cols), bf16),
            pltpu.VMEM((chips, rows, piece), f32),
            pltpu.VMEM((chips, rows, piece), f32),
            pltpu.VMEM(folded, bf16),
            pltpu.VMEM((CHUNKS, groups, 2 * CAP, cols // 2), bf16),
            pltpu.VMEM((rows, hist_rows), bf16),
            pltpu.VMEM((item_rows, rows), bf16),
            dma(7), dma(3 + CHUNKS), dma(2), pltpu.SemaphoreType.REGULAR,
            dma(groups), dma(groups), dma(groups), dma(groups),
            dma(CHUNKS, chips), dma(CHUNKS, chips), dma(chips), dma(chips),
            dma(CHUNKS, chips), dma(CHUNKS, chips), dma(chips), dma(chips),
            dma(groups), dma(groups), dma(CHUNKS, groups), dma(CHUNKS, groups),
        ],
        compiler_params=pltpu.CompilerParams(
            collective_id=0, has_side_effects=True, vmem_limit_bytes=60 * 2**20
        ),
    )(
        item_gain[None, :], history[None, :], owner_map, user_gain[None, :],
        item_hidden, value_weight, value_grad,
    )
    return pl.pallas_call(
        functools.partial(finish, groups),
        out_shape=(
            jax.ShapeDtypeStruct((hist_rows, out_width), bf16),
            jax.ShapeDtypeStruct((item_rows, width), f32),
        ),
        in_specs=[hbm] * 6,
        out_specs=(hbm,) * 2,
        scratch_shapes=[
            pltpu.VMEM(folded, bf16),
            pltpu.VMEM((CHUNKS, groups, 2 * CAP, cols // 2), bf16),
            pltpu.VMEM((rows, hist_rows), bf16),
            pltpu.VMEM((item_rows, rows), bf16),
            pltpu.VMEM((item_rows, width), bf16),
            pltpu.VMEM((1, width), f32),
            pltpu.VMEM((hist_rows, out_width), bf16),
            pltpu.VMEM((item_rows, width), f32),
            dma(6), dma(2),
        ],
        compiler_params=pltpu.CompilerParams(vmem_limit_bytes=60 * 2**20),
    )(back, total, place, select, item_hidden, item_gain[None, :])


def local(item_hidden, item_gain, history, owner_map, user_gain, value_weight, value_grad):
    chips = lax.axis_size("fsdp") // 2
    moved = 2 * chips * lax.axis_size("dp") * CAP
    by_rows = moved <= value_grad.shape[1] and lax.axis_size("dp") * CAP <= 128
    plan = local_moving_rows if by_rows else local_moving_weight
    return plan(
        item_hidden, item_gain, history, owner_map, user_gain, value_weight, value_grad
    )


def solution(mesh):
    in_specs = (
        P(("dp", "fsdp"), None),
        P(),
        P(("dp", "fsdp")),
        P("fsdp", None),
        P(),
        P("fsdp", None),
        P(("dp", "fsdp"), None),
    )
    out_specs = (P(("dp", "fsdp"), None), P(("dp", "fsdp"), None))
    return jax.shard_map(local, mesh=mesh, in_specs=in_specs, out_specs=out_specs, check_vma=False)
```

```python
import functools
import jax
import jax.numpy as jnp
from jax import lax
from jax.experimental import pallas as pl
from jax.experimental.pallas import tpu as pltpu
from jax.sharding import PartitionSpec as P

CAP = 8
MESH = pl.DeviceIdType.MESH
f32 = jnp.float32
bf16 = jnp.bfloat16


eps = 1e-06


def norm_rows(values, gain):
    scale = lax.rsqrt(jnp.mean(values * values, axis=1, keepdims=True) + eps)
    return (values * scale * gain, scale)


def norm_back(values, gain, scale, upstream):
    unit = values * scale
    scaled = upstream * gain
    return scale * (scaled - unit * jnp.mean(scaled * unit, axis=1, keepdims=True))


def locate(owner_row, items):
    matches = items[:, None] == lax.broadcasted_iota(
        jnp.int32, (items.shape[0], owner_row.shape[0]), 1
    )
    return jnp.sum(jnp.where(matches, owner_row[None, :], 0), axis=1)


def local_moving_weight(item_hidden, item_gain, history, owner_map, user_gain, value_weight, value_grad):
    groups = lax.axis_size("dp")
    here = lax.axis_index("dp")
    item_rows = item_hidden.shape[0]
    hist_rows = history.shape[0]
    width = item_hidden.shape[1]
    owner_row = owner_map[0]
    pool = owner_row.shape[0]
    hidden = item_hidden.astype(jnp.float32)
    item_emb, item_scale = norm_rows(hidden, item_gain)
    item_emb = item_emb.astype(jnp.bfloat16)
    all_history = lax.all_gather(history, "dp", axis=0, tiled=True)
    stored_all = locate(owner_row, all_history).reshape(groups, hist_rows)
    local_rows = lax.broadcasted_iota(jnp.int32, (groups, hist_rows, item_rows), 2)
    wanted = jnp.any(stored_all[:, :, None] == here * item_rows + local_rows, axis=1)
    slot = jnp.cumsum(wanted.astype(jnp.int32), axis=1) - 1
    slot_ids = lax.broadcasted_iota(jnp.int32, (groups, CAP, item_rows), 1)
    select = (wanted[:, None, :] & (slot[:, None, :] == slot_ids)).astype(jnp.bfloat16)
    outgoing = jnp.einsum(
        "dcr,rk->dck", select, item_emb, preferred_element_type=jnp.float32
    ).astype(jnp.bfloat16)
    incoming = lax.all_to_all(outgoing, "dp", split_axis=0, concat_axis=0, tiled=True)
    stored = locate(owner_row, history)
    pick = stored[:, None] == lax.broadcasted_iota(jnp.int32, (hist_rows, pool), 1)
    own_wanted = jnp.any(pick, axis=0).reshape(groups, item_rows)
    own_slot = (jnp.cumsum(own_wanted.astype(jnp.int32), axis=1) - 1).reshape(pool)
    slot_pos = jnp.sum(jnp.where(pick, own_slot[None, :], 0), axis=1)
    buffer_row = stored // item_rows * CAP + slot_pos
    x = jnp.take(incoming.reshape(groups * CAP, width), buffer_row, axis=0).astype(jnp.float32)
    normed, scale = norm_rows(x, user_gain)
    normed = normed.astype(jnp.bfloat16)
    whole = lax.all_gather(value_weight, "fsdp", axis=0, tiled=True)
    values = jnp.dot(normed, whole, preferred_element_type=jnp.float32)
    upstream = lax.dot_general(
        value_grad, whole, (((1,), (1,)), ((), ())), preferred_element_type=jnp.float32
    )
    values = values.astype(jnp.bfloat16)
    dx = norm_back(x, user_gain, scale, upstream)
    one_hot = (
        buffer_row[:, None] == lax.broadcasted_iota(jnp.int32, (hist_rows, groups * CAP), 1)
    ).astype(jnp.float32)
    summed = lax.dot_general(
        one_hot,
        dx,
        (((0,), (0,)), ((), ())),
        precision=lax.Precision.HIGHEST,
        preferred_element_type=jnp.float32,
    )
    returned = lax.all_to_all(
        summed.astype(jnp.bfloat16).reshape(groups, CAP, width),
        "dp",
        split_axis=0,
        concat_axis=0,
        tiled=True,
    )
    emb_grad = jnp.einsum("dcr,dck->rk", select, returned, preferred_element_type=jnp.float32)
    item_grad = norm_back(hidden, item_gain, item_scale, emb_grad)
    return (values, item_grad)


CHUNKS = 4


def iota(shape, dim):
    return lax.broadcasted_iota(jnp.int32, shape, dim)


def dot(a, b, ca=1, cb=0):
    return lax.dot_general(a, b, (((ca,), (cb,)), ((), ())), preferred_element_type=f32)


def fold(rows):
    half = rows.shape[1] // 2
    return jnp.concatenate([rows[:, :half], rows[:, half:]], axis=0)


def unfold(rows):
    return jnp.concatenate([rows[:CAP], rows[CAP:]], axis=1)


def stored_rows(hist, parts, item_rows):
    pool = parts.shape[1]
    named = (iota((pool, hist.shape[1]), 0) == hist).astype(f32).astype(bf16)
    found = dot(parts, named)
    return found[0:1] * item_rows + found[1:2]


def slots(wants, item_rows):
    lane = iota((item_rows, 128), 1)
    wanted = jnp.zeros((item_rows, 128), f32)
    for group, want in enumerate(wants):
        wanted = jnp.where(lane // CAP == group, want, wanted)
    before = (iota((item_rows, item_rows), 1) < iota((item_rows, item_rows), 0)).astype(f32)
    slot = dot(before.astype(bf16), wanted.astype(bf16))
    return jnp.where(slot == (lane % CAP).astype(f32), wanted, 0.0)


def kernel(
    groups, chips,
    item_gain_hbm, history_hbm, owner_hbm, user_gain_hbm, item_hidden, weight, value_grad,
    back_in, total_in, place_out, select_out,
    item_gain, history, owner, user_gain,
    hidden_buf, grad_buf, w_buf, hist_buf, emb_out, emb_in, sum_buf, x_out, x_in,
    part_own, part_out, part_in, up_out, up_in, back_out, total_buf, place_buf, select_buf,
    local_sem, out_sem, w_sem, hello, hist_send, hist_recv, emb_send, emb_recv, sum_send, sum_recv,
    x_send, x_recv, part_send, part_recv, up_send, up_recv, back_send, back_recv, total_send, total_recv,
):
    here = lax.axis_index("dp")
    fsdp = lax.axis_index("fsdp")
    chip = fsdp // 2
    core = fsdp % 2
    item_rows, width = item_hidden.shape
    hist_rows = history.shape[1]
    rows = groups * CAP
    piece = width // chips
    cols = value_grad.shape[1] // CHUNKS
    peers = [lax.rem(here + k, groups) for k in range(1, groups)]
    mates = [lax.rem(chip + k, chips) for k in range(1, chips)]

    def dp_id(peer):
        return (peer, fsdp)

    def chip_id(mate):
        return (here, mate * 2 + core)

    sibling = (here, chip * 2 + 1 - core)

    barrier = pltpu.get_barrier_semaphore()
    group = [dp_id(p) for p in peers] + [chip_id(m) for m in mates]
    for target in group:
        pl.semaphore_signal(barrier, inc=1, device_id=target, device_id_type=MESH)

    loads = [
        pltpu.make_async_copy(src, dst, local_sem.at[k])
        for k, (src, dst) in enumerate([
            (history_hbm, history), (owner_hbm, owner), (value_grad, grad_buf),
            (item_hidden, hidden_buf), (item_gain_hbm, item_gain),
            (user_gain_hbm, user_gain), (weight, w_buf.at[core]),
        ])
    ]
    for load in loads:
        load.start()

    @pl.when(core == 0)
    def _():
        pl.semaphore_wait(barrier, len(group))
        pl.semaphore_signal(barrier, inc=1, device_id=sibling, device_id_type=MESH)

    @pl.when(core == 1)
    def _():
        pl.semaphore_wait(barrier, len(group) + 1)
        pl.semaphore_signal(hello, inc=1, device_id=sibling, device_id_type=MESH)

    w_copy = pltpu.make_async_remote_copy(
        src_ref=weight, dst_ref=w_buf.at[core], send_sem=w_sem.at[0], recv_sem=w_sem.at[1],
        device_id=sibling, device_id_type=MESH,
    )

    @pl.when(core == 1)
    def _():
        w_copy.start()

    def remote(src, dst, send, recv, target):
        return pltpu.make_async_remote_copy(
            src_ref=src, dst_ref=dst, send_sem=send, recv_sem=recv,
            device_id=target, device_id_type=MESH,
        )

    sends = []

    def send_dp(out_of, into, send, recv):
        for k, peer in enumerate(peers):
            copy = remote(out_of(peer), into.at[here], send.at[k], recv.at[here], dp_id(peer))
            copy.start()
            sends.append(copy)

    def wait_dp(into, send, recv):
        for k, peer in enumerate(peers):
            remote(into.at[peer], into.at[peer], send.at[k], recv.at[peer], dp_id(peer)).wait_recv()

    def send_chip(out_of, into, send, recv):
        for k, mate in enumerate(mates):
            copy = remote(out_of(mate), into.at[chip], send.at[k], recv.at[chip], chip_id(mate))
            copy.start()
            sends.append(copy)

    def wait_chip(into, send, recv):
        for k, mate in enumerate(mates):
            remote(into.at[mate], into.at[mate], send.at[k], recv.at[mate], chip_id(mate)).wait_recv()

    send_dp(lambda peer: history_hbm, hist_buf, hist_send, hist_recv)
    loads[0].wait()
    hist_buf[here] = history[...]

    loads[1].wait()
    owner_row = owner[...]
    pool = owner_row.shape[1]
    div = (owner_row // item_rows).astype(f32)
    mod = (owner_row % item_rows).astype(f32)
    parts = jnp.where(iota((8, pool), 0) == 0, div, mod).astype(bf16)

    own = stored_rows(history[...], parts, item_rows)
    match = (iota((pool, hist_rows), 0).astype(f32) == own).astype(f32)
    wants = [
        jnp.max(match[e * item_rows : (e + 1) * item_rows], axis=1, keepdims=True)
        for e in range(groups)
    ]
    one_hot = slots(wants, item_rows)
    lane = iota((item_rows, 128), 1)
    stacked = jnp.concatenate(
        [jnp.where(lane // CAP == e, one_hot, 0.0) for e in range(groups)], axis=0
    )
    place = dot(stacked.astype(bf16), match.astype(bf16), 0, 0)[:rows]
    place = place.astype(bf16)
    place_buf[...] = place
    outs = [pltpu.make_async_copy(place_buf, place_out, out_sem.at[0])]
    outs[0].start()

    loads[2].wait()
    for c in range(CHUNKS):
        sum_buf[c, chip] = dot(place, grad_buf[:, c * cols : (c + 1) * cols]).astype(bf16)
        send_chip(
            lambda mate: sum_buf.at[c, chip], sum_buf.at[c], sum_send.at[c], sum_recv.at[c]
        )

    loads[3].wait()
    loads[4].wait()
    hidden = hidden_buf[...].astype(f32)
    item_scale = lax.rsqrt(jnp.mean(hidden * hidden, axis=1, keepdims=True) + 1e-6)
    item_emb = (hidden * item_scale * item_gain[...]).astype(bf16)
    loads[5].wait()
    held = item_emb.astype(f32)
    held_scale = lax.rsqrt(jnp.mean(held * held, axis=1, keepdims=True) + 1e-6)
    held_normed = (held * held_scale * user_gain[...]).astype(bf16)

    wait_dp(hist_buf, hist_send, hist_recv)
    base = (here * item_rows).astype(f32)
    local_rows = iota((item_rows, hist_rows), 0).astype(f32) + base
    wants = []
    for t in range(groups):
        stored = stored_rows(hist_buf[t], parts, item_rows)
        wants.append(jnp.max((local_rows == stored).astype(f32), axis=1, keepdims=True))
    select = slots(wants, item_rows)[:, :rows].astype(bf16)
    select_buf[...] = select
    outs.append(pltpu.make_async_copy(select_buf, select_out, out_sem.at[1]))
    outs[1].start()
    normed = dot(select, held_normed, 0, 0).astype(bf16)
    for p in range(chips):
        x_out[p] = normed[:, p * piece : (p + 1) * piece]
    send_chip(lambda mate: x_out.at[mate], x_in, x_send, x_recv)
    x_in[chip] = x_out[chip]
    outgoing = dot(select, item_emb, 0, 0)
    for t in range(groups):
        emb_out[t] = fold(outgoing[t * CAP : (t + 1) * CAP]).astype(bf16)
    send_dp(lambda peer: emb_out.at[peer], emb_in, emb_send, emb_recv)
    emb_in[here] = emb_out[here]

    @pl.when(core == 0)
    def _():
        pl.semaphore_wait(hello, 1)
        w_copy.start()

    loads[6].wait()
    w_copy.wait()
    w_all = w_buf[...].reshape(piece, -1)

    def send_part(c):
        part = dot(x_all, w_all[:, c * cols : (c + 1) * cols]).reshape(chips, rows, cols)
        part_own[c] = part
        part_out[c] = part.astype(bf16)
        send_chip(
            lambda mate: part_out.at[c, mate], part_in.at[c], part_send.at[c], part_recv.at[c]
        )

    def send_total(c):
        wait_chip(part_in.at[c], part_send.at[c], part_recv.at[c])
        total = part_own[c, chip]
        for mate in mates:
            total = total + part_in[c, mate].astype(f32)
        for t in range(groups):
            total_buf[c, t] = fold(total[t * CAP : (t + 1) * CAP]).astype(bf16)
        send_dp(
            lambda peer: total_buf.at[c, peer], total_in.at[c], total_send.at[c], total_recv.at[c]
        )
        out = pltpu.make_async_copy(
            total_buf.at[c, here], total_in.at[c, here], out_sem.at[3 + c]
        )
        out.start()
        outs.append(out)

    wait_chip(x_in, x_send, x_recv)
    x_all = x_in[...].reshape(chips * rows, piece)
    for c in range(CHUNKS // 2):
        send_part(c)

    up = jnp.zeros((chips * rows, piece), f32)
    for c in range(CHUNKS):
        wait_chip(sum_buf.at[c], sum_send.at[c], sum_recv.at[c])
        sums = sum_buf[c].reshape(chips * rows, cols)
        up = up + dot(sums, w_all[:, c * cols : (c + 1) * cols], 1, 1)
    up_out[...] = up.reshape(chips, rows, piece)
    send_chip(lambda mate: up_out.at[mate], up_in, up_send, up_recv)
    up_in[chip] = up_out[chip]

    for c in range(CHUNKS // 2, CHUNKS):
        send_part(c)
    for c in range(CHUNKS // 2):
        send_total(c)

    wait_dp(emb_in, emb_send, emb_recv)
    x = jnp.concatenate([unfold(emb_in[e].astype(f32)) for e in range(groups)], axis=0)
    scale = lax.rsqrt(jnp.mean(x * x, axis=1, keepdims=True) + 1e-6)
    wait_chip(up_in, up_send, up_recv)
    upstream = jnp.concatenate([up_in[p] for p in range(chips)], axis=1)
    unit = x * scale
    scaled = upstream * user_gain[...]
    block_sum = scale * (scaled - unit * jnp.mean(scaled * unit, axis=1, keepdims=True))
    for t in range(groups):
        back_out[t] = fold(block_sum[t * CAP : (t + 1) * CAP]).astype(bf16)
    send_dp(lambda peer: back_out.at[peer], back_in, back_send, back_recv)
    outs.append(pltpu.make_async_copy(back_out.at[here], back_in.at[here], out_sem.at[2]))
    outs[-1].start()
    for c in range(CHUNKS // 2, CHUNKS):
        send_total(c)

    wait_dp(back_in, back_send, back_recv)
    for c in range(CHUNKS):
        wait_dp(total_in.at[c], total_send.at[c], total_recv.at[c])
    for out in outs:
        out.wait()
    for copy in sends:
        copy.wait_send()


def finish(
    groups, back_hbm, total_hbm, place_hbm, select_hbm, hidden_hbm, gain_hbm,
    values_out, item_grad_out,
    back, total, place, select, hidden_buf, gain, values, item_grad, load_sem, out_sem,
):
    loads = [
        pltpu.make_async_copy(src, dst, load_sem.at[k])
        for k, (src, dst) in enumerate([
            (hidden_hbm, hidden_buf), (gain_hbm, gain), (select_hbm, select), (back_hbm, back),
            (place_hbm, place), (total_hbm, total),
        ])
    ]
    for load in loads:
        load.start()
    loads[0].wait()
    loads[1].wait()
    hidden = hidden_buf[...].astype(f32)
    scale = lax.rsqrt(jnp.mean(hidden * hidden, axis=1, keepdims=True) + 1e-6)
    loads[2].wait()
    loads[3].wait()
    returned = jnp.concatenate([unfold(back[t].astype(f32)) for t in range(groups)], axis=0)
    emb_grad = dot(select[...], returned.astype(bf16))
    unit = hidden * scale
    scaled = emb_grad * gain[...]
    item_grad[...] = scale * (scaled - unit * jnp.mean(scaled * unit, axis=1, keepdims=True))
    grad_copy = pltpu.make_async_copy(item_grad, item_grad_out, out_sem.at[0])
    grad_copy.start()
    loads[4].wait()
    loads[5].wait()
    named = place[...]
    cols = values.shape[1] // CHUNKS
    for c in range(CHUNKS):
        rows = [unfold(total[c, e].astype(f32)) for e in range(groups)]
        rows = jnp.concatenate(rows, axis=0).astype(bf16)
        values[:, c * cols : (c + 1) * cols] = dot(named, rows, 0, 0).astype(bf16)
    values_copy = pltpu.make_async_copy(values, values_out, out_sem.at[1])
    values_copy.start()
    grad_copy.wait()
    values_copy.wait()


def local_moving_rows(
    item_hidden, item_gain, history, owner_map, user_gain, value_weight, value_grad
):
    groups = lax.axis_size("dp")
    chips = lax.axis_size("fsdp") // 2
    item_rows, width = item_hidden.shape
    hist_rows, out_width = value_grad.shape
    rows = groups * CAP
    depth = value_weight.shape[0]
    piece = 2 * depth
    cols = out_width // CHUNKS
    hbm = pl.BlockSpec(memory_space=pl.ANY)

    def dma(*counts):
        return pltpu.SemaphoreType.DMA(counts)

    folded = (groups, 2 * CAP, width // 2)
    back, total, place, select = pl.pallas_call(
        functools.partial(kernel, groups, chips),
        out_shape=(
            jax.ShapeDtypeStruct(folded, bf16),
            jax.ShapeDtypeStruct((CHUNKS, groups, 2 * CAP, cols // 2), bf16),
            jax.ShapeDtypeStruct((rows, hist_rows), bf16),
            jax.ShapeDtypeStruct((item_rows, rows), bf16),
        ),
        in_specs=[hbm] * 7,
        out_specs=(hbm,) * 4,
        scratch_shapes=[
            pltpu.VMEM((1, width), f32),
            pltpu.VMEM((1, hist_rows), jnp.int32),
            pltpu.VMEM((1, owner_map.shape[1]), jnp.int32),
            pltpu.VMEM((1, width), f32),
            pltpu.VMEM((item_rows, width), bf16),
            pltpu.VMEM((hist_rows, out_width), bf16),
            pltpu.VMEM((2, depth, out_width), bf16),
            pltpu.VMEM((groups, 1, hist_rows), jnp.int32),
            pltpu.VMEM(folded, bf16),
            pltpu.VMEM(folded, bf16),
            pltpu.VMEM((CHUNKS, chips, rows, cols), bf16),
            pltpu.VMEM((chips, rows, piece), bf16),
            pltpu.VMEM((chips, rows, piece), bf16),
            pltpu.VMEM((CHUNKS, chips, rows, cols), f32),
            pltpu.VMEM((CHUNKS, chips, rows, cols), bf16),
            pltpu.VMEM((CHUNKS, chips, rows, cols), bf16),
            pltpu.VMEM((chips, rows, piece), f32),
            pltpu.VMEM((chips, rows, piece), f32),
            pltpu.VMEM(folded, bf16),
            pltpu.VMEM((CHUNKS, groups, 2 * CAP, cols // 2), bf16),
            pltpu.VMEM((rows, hist_rows), bf16),
            pltpu.VMEM((item_rows, rows), bf16),
            dma(7), dma(3 + CHUNKS), dma(2), pltpu.SemaphoreType.REGULAR,
            dma(groups), dma(groups), dma(groups), dma(groups),
            dma(CHUNKS, chips), dma(CHUNKS, chips), dma(chips), dma(chips),
            dma(CHUNKS, chips), dma(CHUNKS, chips), dma(chips), dma(chips),
            dma(groups), dma(groups), dma(CHUNKS, groups), dma(CHUNKS, groups),
        ],
        compiler_params=pltpu.CompilerParams(
            collective_id=0, has_side_effects=True, vmem_limit_bytes=60 * 2**20
        ),
    )(
        item_gain[None, :], history[None, :], owner_map, user_gain[None, :],
        item_hidden, value_weight, value_grad,
    )
    return pl.pallas_call(
        functools.partial(finish, groups),
        out_shape=(
            jax.ShapeDtypeStruct((hist_rows, out_width), bf16),
            jax.ShapeDtypeStruct((item_rows, width), f32),
        ),
        in_specs=[hbm] * 6,
        out_specs=(hbm,) * 2,
        scratch_shapes=[
            pltpu.VMEM(folded, bf16),
            pltpu.VMEM((CHUNKS, groups, 2 * CAP, cols // 2), bf16),
            pltpu.VMEM((rows, hist_rows), bf16),
            pltpu.VMEM((item_rows, rows), bf16),
            pltpu.VMEM((item_rows, width), bf16),
            pltpu.VMEM((1, width), f32),
            pltpu.VMEM((hist_rows, out_width), bf16),
            pltpu.VMEM((item_rows, width), f32),
            dma(6), dma(2),
        ],
        compiler_params=pltpu.CompilerParams(vmem_limit_bytes=60 * 2**20),
    )(back, total, place, select, item_hidden, item_gain[None, :])


def local(item_hidden, item_gain, history, owner_map, user_gain, value_weight, value_grad):
    chips = lax.axis_size("fsdp") // 2
    moved = 2 * chips * lax.axis_size("dp") * CAP
    by_rows = moved <= value_grad.shape[1] and lax.axis_size("dp") * CAP <= 128
    plan = local_moving_rows if by_rows else local_moving_weight
    return plan(
        item_hidden, item_gain, history, owner_map, user_gain, value_weight, value_grad
    )


def solution(mesh):
    in_specs = (
        P(("dp", "fsdp"), None),
        P(),
        P(("dp", "fsdp")),
        P("fsdp", None),
        P(),
        P("fsdp", None),
        P(("dp", "fsdp"), None),
    )
    out_specs = (P(("dp", "fsdp"), None), P(("dp", "fsdp"), None))
    return jax.shard_map(local, mesh=mesh, in_specs=in_specs, out_specs=out_specs, check_vma=False)
```

```python
import functools
import jax
import jax.numpy as jnp
from jax import lax
from jax.experimental import pallas as pl
from jax.experimental.pallas import tpu as pltpu
from jax.sharding import PartitionSpec as P

CAP = 8
MESH = pl.DeviceIdType.MESH
f32 = jnp.float32
bf16 = jnp.bfloat16


eps = 1e-06


def norm_rows(values, gain):
    scale = lax.rsqrt(jnp.mean(values * values, axis=1, keepdims=True) + eps)
    return (values * scale * gain, scale)


def norm_back(values, gain, scale, upstream):
    unit = values * scale
    scaled = upstream * gain
    return scale * (scaled - unit * jnp.mean(scaled * unit, axis=1, keepdims=True))


def locate(owner_row, items):
    matches = items[:, None] == lax.broadcasted_iota(
        jnp.int32, (items.shape[0], owner_row.shape[0]), 1
    )
    return jnp.sum(jnp.where(matches, owner_row[None, :], 0), axis=1)


def local_moving_weight(item_hidden, item_gain, history, owner_map, user_gain, value_weight, value_grad):
    groups = lax.axis_size("dp")
    here = lax.axis_index("dp")
    item_rows = item_hidden.shape[0]
    hist_rows = history.shape[0]
    width = item_hidden.shape[1]
    owner_row = owner_map[0]
    pool = owner_row.shape[0]
    hidden = item_hidden.astype(jnp.float32)
    item_emb, item_scale = norm_rows(hidden, item_gain)
    item_emb = item_emb.astype(jnp.bfloat16)
    all_history = lax.all_gather(history, "dp", axis=0, tiled=True)
    stored_all = locate(owner_row, all_history).reshape(groups, hist_rows)
    local_rows = lax.broadcasted_iota(jnp.int32, (groups, hist_rows, item_rows), 2)
    wanted = jnp.any(stored_all[:, :, None] == here * item_rows + local_rows, axis=1)
    slot = jnp.cumsum(wanted.astype(jnp.int32), axis=1) - 1
    slot_ids = lax.broadcasted_iota(jnp.int32, (groups, CAP, item_rows), 1)
    select = (wanted[:, None, :] & (slot[:, None, :] == slot_ids)).astype(jnp.bfloat16)
    outgoing = jnp.einsum(
        "dcr,rk->dck", select, item_emb, preferred_element_type=jnp.float32
    ).astype(jnp.bfloat16)
    incoming = lax.all_to_all(outgoing, "dp", split_axis=0, concat_axis=0, tiled=True)
    stored = locate(owner_row, history)
    pick = stored[:, None] == lax.broadcasted_iota(jnp.int32, (hist_rows, pool), 1)
    own_wanted = jnp.any(pick, axis=0).reshape(groups, item_rows)
    own_slot = (jnp.cumsum(own_wanted.astype(jnp.int32), axis=1) - 1).reshape(pool)
    slot_pos = jnp.sum(jnp.where(pick, own_slot[None, :], 0), axis=1)
    buffer_row = stored // item_rows * CAP + slot_pos
    x = jnp.take(incoming.reshape(groups * CAP, width), buffer_row, axis=0).astype(jnp.float32)
    normed, scale = norm_rows(x, user_gain)
    normed = normed.astype(jnp.bfloat16)
    whole = lax.all_gather(value_weight, "fsdp", axis=0, tiled=True)
    values = jnp.dot(normed, whole, preferred_element_type=jnp.float32)
    upstream = lax.dot_general(
        value_grad, whole, (((1,), (1,)), ((), ())), preferred_element_type=jnp.float32
    )
    values = values.astype(jnp.bfloat16)
    dx = norm_back(x, user_gain, scale, upstream)
    one_hot = (
        buffer_row[:, None] == lax.broadcasted_iota(jnp.int32, (hist_rows, groups * CAP), 1)
    ).astype(jnp.float32)
    summed = lax.dot_general(
        one_hot,
        dx,
        (((0,), (0,)), ((), ())),
        precision=lax.Precision.HIGHEST,
        preferred_element_type=jnp.float32,
    )
    returned = lax.all_to_all(
        summed.astype(jnp.bfloat16).reshape(groups, CAP, width),
        "dp",
        split_axis=0,
        concat_axis=0,
        tiled=True,
    )
    emb_grad = jnp.einsum("dcr,dck->rk", select, returned, preferred_element_type=jnp.float32)
    item_grad = norm_back(hidden, item_gain, item_scale, emb_grad)
    return (values, item_grad)


CHUNKS = 2


def iota(shape, dim):
    return lax.broadcasted_iota(jnp.int32, shape, dim)


def dot(a, b, ca=1, cb=0):
    return lax.dot_general(a, b, (((ca,), (cb,)), ((), ())), preferred_element_type=f32)


def fold(rows):
    half = rows.shape[1] // 2
    return jnp.concatenate([rows[:, :half], rows[:, half:]], axis=0)


def unfold(rows):
    return jnp.concatenate([rows[:CAP], rows[CAP:]], axis=1)


def stored_rows(hist, parts, item_rows):
    pool = parts.shape[1]
    named = (iota((pool, hist.shape[1]), 0) == hist).astype(f32).astype(bf16)
    found = dot(parts, named)
    return found[0:1] * item_rows + found[1:2]


def slots(wants, item_rows):
    lane = iota((item_rows, 128), 1)
    wanted = jnp.zeros((item_rows, 128), f32)
    for group, want in enumerate(wants):
        wanted = jnp.where(lane // CAP == group, want, wanted)
    before = (iota((item_rows, item_rows), 1) < iota((item_rows, item_rows), 0)).astype(f32)
    slot = dot(before.astype(bf16), wanted.astype(bf16))
    return jnp.where(slot == (lane % CAP).astype(f32), wanted, 0.0)


def kernel(
    groups, chips,
    item_gain_hbm, history_hbm, owner_hbm, user_gain_hbm, item_hidden, weight, value_grad,
    back_in, total_out, place_out, select_out,
    item_gain, history, owner, user_gain,
    hidden_buf, grad_buf, w_buf, hist_buf, emb_out, emb_in, sum_buf, x_out, x_in,
    part_own, part_out, part_in, back_out, total_buf, place_buf, select_buf,
    local_sem, out_sem, w_sem, hello, hist_send, hist_recv, emb_send, emb_recv, sum_send, sum_recv,
    x_send, x_recv, part_send, part_recv, back_send, back_recv,
):
    here = lax.axis_index("dp")
    fsdp = lax.axis_index("fsdp")
    chip = fsdp // 2
    core = fsdp % 2
    item_rows, width = item_hidden.shape
    hist_rows = history.shape[1]
    rows = groups * CAP
    piece = width // chips
    cols = value_grad.shape[1] // CHUNKS
    peers = [lax.rem(here + k, groups) for k in range(1, groups)]
    mates = [lax.rem(chip + k, chips) for k in range(1, chips)]

    def dp_id(peer):
        return (peer, fsdp)

    def chip_id(mate):
        return (here, mate * 2 + core)

    sibling = (here, chip * 2 + 1 - core)

    barrier = pltpu.get_barrier_semaphore()
    others = [
        (lax.rem(here + i, groups), lax.rem(chip + j, chips))
        for i in range(groups) for j in range(chips) if i or j
    ]
    group = [(peer, mate * 2 + core) for peer, mate in others]
    for target in group:
        pl.semaphore_signal(barrier, inc=1, device_id=target, device_id_type=MESH)

    loads = [
        pltpu.make_async_copy(src, dst, local_sem.at[k])
        for k, (src, dst) in enumerate([
            (history_hbm, history), (owner_hbm, owner), (value_grad, grad_buf),
            (item_hidden, hidden_buf), (item_gain_hbm, item_gain),
            (user_gain_hbm, user_gain), (weight, w_buf.at[core]),
        ])
    ]
    for load in loads:
        load.start()

    @pl.when(core == 0)
    def _():
        pl.semaphore_wait(barrier, len(group))
        pl.semaphore_signal(barrier, inc=1, device_id=sibling, device_id_type=MESH)

    @pl.when(core == 1)
    def _():
        pl.semaphore_wait(barrier, len(group) + 1)
        pl.semaphore_signal(hello, inc=1, device_id=sibling, device_id_type=MESH)

    w_copy = pltpu.make_async_remote_copy(
        src_ref=weight, dst_ref=w_buf.at[core], send_sem=w_sem.at[0], recv_sem=w_sem.at[1],
        device_id=sibling, device_id_type=MESH,
    )

    @pl.when(core == 1)
    def _():
        w_copy.start()

    def remote(src, dst, send, recv, target):
        return pltpu.make_async_remote_copy(
            src_ref=src, dst_ref=dst, send_sem=send, recv_sem=recv,
            device_id=target, device_id_type=MESH,
        )

    sends = []

    def send_dp(out_of, into, send, recv):
        for k, peer in enumerate(peers):
            copy = remote(out_of(peer), into.at[here], send.at[k], recv.at[here], dp_id(peer))
            copy.start()
            sends.append(copy)

    def wait_dp(into, send, recv):
        for k, peer in enumerate(peers):
            remote(into.at[peer], into.at[peer], send.at[k], recv.at[peer], dp_id(peer)).wait_recv()

    def send_chip(out_of, into, send, recv):
        for k, mate in enumerate(mates):
            copy = remote(out_of(mate), into.at[chip], send.at[k], recv.at[chip], chip_id(mate))
            copy.start()
            sends.append(copy)

    def wait_chip(into, send, recv):
        for k, mate in enumerate(mates):
            remote(into.at[mate], into.at[mate], send.at[k], recv.at[mate], chip_id(mate)).wait_recv()

    send_dp(lambda peer: history_hbm, hist_buf, hist_send, hist_recv)
    loads[0].wait()
    hist_buf[here] = history[...]

    loads[1].wait()
    owner_row = owner[...]
    pool = owner_row.shape[1]
    div = (owner_row // item_rows).astype(f32)
    mod = (owner_row % item_rows).astype(f32)
    parts = jnp.where(iota((8, pool), 0) == 0, div, mod).astype(bf16)

    own = stored_rows(history[...], parts, item_rows)
    match = (iota((pool, hist_rows), 0).astype(f32) == own).astype(f32)
    wants = [
        jnp.max(match[e * item_rows : (e + 1) * item_rows], axis=1, keepdims=True)
        for e in range(groups)
    ]
    one_hot = slots(wants, item_rows)
    lane = iota((item_rows, 128), 1)
    stacked = jnp.concatenate(
        [jnp.where(lane // CAP == e, one_hot, 0.0) for e in range(groups)], axis=0
    )
    place = dot(stacked.astype(bf16), match.astype(bf16), 0, 0)[:rows]
    place = place.astype(bf16)
    place_buf[...] = place
    outs = [pltpu.make_async_copy(place_buf, place_out, out_sem.at[0])]
    outs[0].start()

    loads[2].wait()
    for c in range(CHUNKS):
        sum_buf[c, chip] = dot(place, grad_buf[:, c * cols : (c + 1) * cols]).astype(bf16)
        send_chip(
            lambda mate: sum_buf.at[c, chip], sum_buf.at[c], sum_send.at[c], sum_recv.at[c]
        )

    loads[3].wait()
    loads[4].wait()
    hidden = hidden_buf[...].astype(f32)
    item_scale = lax.rsqrt(jnp.mean(hidden * hidden, axis=1, keepdims=True) + 1e-6)
    item_emb = (hidden * item_scale * item_gain[...]).astype(bf16)

    wait_dp(hist_buf, hist_send, hist_recv)
    base = (here * item_rows).astype(f32)
    local_rows = iota((item_rows, hist_rows), 0).astype(f32) + base
    wants = []
    for t in range(groups):
        stored = stored_rows(hist_buf[t], parts, item_rows)
        wants.append(jnp.max((local_rows == stored).astype(f32), axis=1, keepdims=True))
    select = slots(wants, item_rows)[:, :rows].astype(bf16)
    select_buf[...] = select
    outs.append(pltpu.make_async_copy(select_buf, select_out, out_sem.at[1]))
    outs[1].start()
    outgoing = dot(select, item_emb, 0, 0)
    for t in range(groups):
        emb_out[t] = fold(outgoing[t * CAP : (t + 1) * CAP]).astype(bf16)
    send_dp(lambda peer: emb_out.at[peer], emb_in, emb_send, emb_recv)
    emb_in[here] = emb_out[here]

    @pl.when(core == 0)
    def _():
        pl.semaphore_wait(hello, 1)
        w_copy.start()

    loads[5].wait()
    wait_dp(emb_in, emb_send, emb_recv)

    x = jnp.concatenate([unfold(emb_in[e].astype(f32)) for e in range(groups)], axis=0)
    scale = lax.rsqrt(jnp.mean(x * x, axis=1, keepdims=True) + 1e-6)
    normed = (x * scale * user_gain[...]).astype(bf16)
    for p in range(chips):
        x_out[p] = normed[:, p * piece : (p + 1) * piece]
    send_chip(lambda mate: x_out.at[mate], x_in, x_send, x_recv)
    x_in[chip] = x_out[chip]

    loads[6].wait()
    w_copy.wait()
    w_all = w_buf[...].reshape(piece, -1)

    up = jnp.zeros((chips * rows, piece), f32)
    for c in range(CHUNKS):
        wait_chip(sum_buf.at[c], sum_send.at[c], sum_recv.at[c])
        sums = sum_buf[c].reshape(chips * rows, cols)
        up = up + dot(sums, w_all[:, c * cols : (c + 1) * cols], 1, 1)
    for m in range(chips):
        for e in range(groups):
            at = m * rows + e * CAP
            back_out[e, m] = fold(up[at : at + CAP]).astype(bf16)
    for peer, mate in others:
        copy = remote(
            back_out.at[peer, mate], back_in.at[here, chip],
            back_send.at[peer, mate], back_recv.at[here, chip], (peer, mate * 2 + core),
        )
        copy.start()
        sends.append(copy)
    outs.append(pltpu.make_async_copy(
        back_out.at[here, chip], back_in.at[here, chip], out_sem.at[2]
    ))
    outs[2].start()

    wait_chip(x_in, x_send, x_recv)
    x_all = x_in[...].reshape(chips * rows, piece)
    for c in range(CHUNKS):
        part = dot(x_all, w_all[:, c * cols : (c + 1) * cols]).reshape(chips, rows, cols)
        part_own[c] = part
        part_out[c] = part.astype(bf16)
        send_chip(
            lambda mate: part_out.at[c, mate], part_in.at[c], part_send.at[c], part_recv.at[c]
        )

    for c in range(CHUNKS):
        wait_chip(part_in.at[c], part_send.at[c], part_recv.at[c])
        total = part_own[c, chip]
        for mate in mates:
            total = total + part_in[c, mate].astype(f32)
        total_buf[c] = total.astype(bf16)
        out = pltpu.make_async_copy(total_buf.at[c], total_out.at[c], out_sem.at[3 + c])
        out.start()
        outs.append(out)

    for peer, mate in others:
        remote(
            back_in.at[peer, mate], back_in.at[peer, mate],
            back_send.at[peer, mate], back_recv.at[peer, mate], (peer, mate * 2 + core),
        ).wait_recv()
    for out in outs:
        out.wait()
    for copy in sends:
        copy.wait_send()


def finish(
    groups, chips,
    back_hbm, total_hbm, place_hbm, select_hbm, hidden_hbm, gain_hbm, user_gain_hbm,
    values_out, item_grad_out,
    back, total, place, select, hidden_buf, gain, user_gain, values, item_grad, load_sem, out_sem,
):
    loads = [
        pltpu.make_async_copy(src, dst, load_sem.at[k])
        for k, (src, dst) in enumerate([
            (hidden_hbm, hidden_buf), (gain_hbm, gain), (select_hbm, select), (back_hbm, back),
            (place_hbm, place), (total_hbm, total), (user_gain_hbm, user_gain),
        ])
    ]
    for load in loads:
        load.start()
    loads[0].wait()
    loads[1].wait()
    hidden = hidden_buf[...].astype(f32)
    scale = lax.rsqrt(jnp.mean(hidden * hidden, axis=1, keepdims=True) + 1e-6)
    unit = hidden * scale
    emb = (unit * gain[...]).astype(bf16).astype(f32)
    emb_scale = lax.rsqrt(jnp.mean(emb * emb, axis=1, keepdims=True) + 1e-6)
    emb_unit = emb * emb_scale
    for load in (loads[2], loads[3], loads[6]):
        load.wait()
    returned = jnp.concatenate([
        jnp.concatenate([unfold(back[t, q].astype(f32)) for q in range(chips)], axis=1)
        for t in range(groups)
    ], axis=0)
    scaled = dot(select[...], returned.astype(bf16)) * user_gain[...]
    emb_grad = emb_scale * (
        scaled - emb_unit * jnp.mean(scaled * emb_unit, axis=1, keepdims=True)
    )
    scaled = emb_grad * gain[...]
    item_grad[...] = scale * (scaled - unit * jnp.mean(scaled * unit, axis=1, keepdims=True))
    grad_copy = pltpu.make_async_copy(item_grad, item_grad_out, out_sem.at[0])
    grad_copy.start()
    loads[4].wait()
    loads[5].wait()
    named = place[...]
    cols = total.shape[2]
    for c in range(CHUNKS):
        values[:, c * cols : (c + 1) * cols] = dot(named, total[c], 0, 0).astype(bf16)
    values_copy = pltpu.make_async_copy(values, values_out, out_sem.at[1])
    values_copy.start()
    grad_copy.wait()
    values_copy.wait()


def local_moving_rows(
    item_hidden, item_gain, history, owner_map, user_gain, value_weight, value_grad
):
    groups = lax.axis_size("dp")
    chips = lax.axis_size("fsdp") // 2
    item_rows, width = item_hidden.shape
    hist_rows, out_width = value_grad.shape
    rows = groups * CAP
    depth = value_weight.shape[0]
    piece = 2 * depth
    cols = out_width // CHUNKS
    hbm = pl.BlockSpec(memory_space=pl.ANY)

    def dma(*counts):
        return pltpu.SemaphoreType.DMA(counts)

    folded = (groups, 2 * CAP, width // 2)
    slices = (groups, chips, 2 * CAP, piece // 2)
    back, total, place, select = pl.pallas_call(
        functools.partial(kernel, groups, chips),
        out_shape=(
            jax.ShapeDtypeStruct(slices, bf16),
            jax.ShapeDtypeStruct((CHUNKS, rows, cols), bf16),
            jax.ShapeDtypeStruct((rows, hist_rows), bf16),
            jax.ShapeDtypeStruct((item_rows, rows), bf16),
        ),
        in_specs=[hbm] * 7,
        out_specs=(hbm,) * 4,
        scratch_shapes=[
            pltpu.VMEM((1, width), f32),
            pltpu.VMEM((1, hist_rows), jnp.int32),
            pltpu.VMEM((1, owner_map.shape[1]), jnp.int32),
            pltpu.VMEM((1, width), f32),
            pltpu.VMEM((item_rows, width), bf16),
            pltpu.VMEM((hist_rows, out_width), bf16),
            pltpu.VMEM((2, depth, out_width), bf16),
            pltpu.VMEM((groups, 1, hist_rows), jnp.int32),
            pltpu.VMEM(folded, bf16),
            pltpu.VMEM(folded, bf16),
            pltpu.VMEM((CHUNKS, chips, rows, cols), bf16),
            pltpu.VMEM((chips, rows, piece), bf16),
            pltpu.VMEM((chips, rows, piece), bf16),
            pltpu.VMEM((CHUNKS, chips, rows, cols), f32),
            pltpu.VMEM((CHUNKS, chips, rows, cols), bf16),
            pltpu.VMEM((CHUNKS, chips, rows, cols), bf16),
            pltpu.VMEM(slices, bf16),
            pltpu.VMEM((CHUNKS, rows, cols), bf16),
            pltpu.VMEM((rows, hist_rows), bf16),
            pltpu.VMEM((item_rows, rows), bf16),
            dma(7), dma(3 + CHUNKS), dma(2), pltpu.SemaphoreType.REGULAR,
            dma(groups), dma(groups), dma(groups), dma(groups),
            dma(CHUNKS, chips), dma(CHUNKS, chips), dma(chips), dma(chips),
            dma(CHUNKS, chips), dma(CHUNKS, chips), dma(groups, chips), dma(groups, chips),
        ],
        compiler_params=pltpu.CompilerParams(
            collective_id=0, has_side_effects=True, vmem_limit_bytes=60 * 2**20
        ),
    )(
        item_gain[None, :], history[None, :], owner_map, user_gain[None, :],
        item_hidden, value_weight, value_grad,
    )
    return pl.pallas_call(
        functools.partial(finish, groups, chips),
        out_shape=(
            jax.ShapeDtypeStruct((hist_rows, out_width), bf16),
            jax.ShapeDtypeStruct((item_rows, width), f32),
        ),
        in_specs=[hbm] * 7,
        out_specs=(hbm,) * 2,
        scratch_shapes=[
            pltpu.VMEM(slices, bf16),
            pltpu.VMEM((CHUNKS, rows, cols), bf16),
            pltpu.VMEM((rows, hist_rows), bf16),
            pltpu.VMEM((item_rows, rows), bf16),
            pltpu.VMEM((item_rows, width), bf16),
            pltpu.VMEM((1, width), f32),
            pltpu.VMEM((1, width), f32),
            pltpu.VMEM((hist_rows, out_width), bf16),
            pltpu.VMEM((item_rows, width), f32),
            dma(7), dma(2),
        ],
        compiler_params=pltpu.CompilerParams(vmem_limit_bytes=60 * 2**20),
    )(back, total, place, select, item_hidden, item_gain[None, :], user_gain[None, :])


def local(item_hidden, item_gain, history, owner_map, user_gain, value_weight, value_grad):
    chips = lax.axis_size("fsdp") // 2
    moved = 2 * chips * lax.axis_size("dp") * CAP
    by_rows = moved <= value_grad.shape[1] and lax.axis_size("dp") * CAP <= 128
    plan = local_moving_rows if by_rows else local_moving_weight
    return plan(
        item_hidden, item_gain, history, owner_map, user_gain, value_weight, value_grad
    )


def solution(mesh):
    in_specs = (
        P(("dp", "fsdp"), None),
        P(),
        P(("dp", "fsdp")),
        P("fsdp", None),
        P(),
        P("fsdp", None),
        P(("dp", "fsdp"), None),
    )
    out_specs = (P(("dp", "fsdp"), None), P(("dp", "fsdp"), None))
    return jax.shard_map(local, mesh=mesh, in_specs=in_specs, out_specs=out_specs, check_vma=False)
```

```python
import functools
import jax
import jax.numpy as jnp
from jax import lax
from jax.experimental import pallas as pl
from jax.experimental.pallas import tpu as pltpu
from jax.sharding import PartitionSpec as P

CAP = 8
MESH = pl.DeviceIdType.MESH
f32 = jnp.float32
bf16 = jnp.bfloat16


eps = 1e-06


def norm_rows(values, gain):
    scale = lax.rsqrt(jnp.mean(values * values, axis=1, keepdims=True) + eps)
    return (values * scale * gain, scale)


def norm_back(values, gain, scale, upstream):
    unit = values * scale
    scaled = upstream * gain
    return scale * (scaled - unit * jnp.mean(scaled * unit, axis=1, keepdims=True))


def locate(owner_row, items):
    matches = items[:, None] == lax.broadcasted_iota(
        jnp.int32, (items.shape[0], owner_row.shape[0]), 1
    )
    return jnp.sum(jnp.where(matches, owner_row[None, :], 0), axis=1)


def local_moving_weight(item_hidden, item_gain, history, owner_map, user_gain, value_weight, value_grad):
    groups = lax.axis_size("dp")
    here = lax.axis_index("dp")
    item_rows = item_hidden.shape[0]
    hist_rows = history.shape[0]
    width = item_hidden.shape[1]
    owner_row = owner_map[0]
    pool = owner_row.shape[0]
    hidden = item_hidden.astype(jnp.float32)
    item_emb, item_scale = norm_rows(hidden, item_gain)
    item_emb = item_emb.astype(jnp.bfloat16)
    all_history = lax.all_gather(history, "dp", axis=0, tiled=True)
    stored_all = locate(owner_row, all_history).reshape(groups, hist_rows)
    local_rows = lax.broadcasted_iota(jnp.int32, (groups, hist_rows, item_rows), 2)
    wanted = jnp.any(stored_all[:, :, None] == here * item_rows + local_rows, axis=1)
    slot = jnp.cumsum(wanted.astype(jnp.int32), axis=1) - 1
    slot_ids = lax.broadcasted_iota(jnp.int32, (groups, CAP, item_rows), 1)
    select = (wanted[:, None, :] & (slot[:, None, :] == slot_ids)).astype(jnp.bfloat16)
    outgoing = jnp.einsum(
        "dcr,rk->dck", select, item_emb, preferred_element_type=jnp.float32
    ).astype(jnp.bfloat16)
    incoming = lax.all_to_all(outgoing, "dp", split_axis=0, concat_axis=0, tiled=True)
    stored = locate(owner_row, history)
    pick = stored[:, None] == lax.broadcasted_iota(jnp.int32, (hist_rows, pool), 1)
    own_wanted = jnp.any(pick, axis=0).reshape(groups, item_rows)
    own_slot = (jnp.cumsum(own_wanted.astype(jnp.int32), axis=1) - 1).reshape(pool)
    slot_pos = jnp.sum(jnp.where(pick, own_slot[None, :], 0), axis=1)
    buffer_row = stored // item_rows * CAP + slot_pos
    x = jnp.take(incoming.reshape(groups * CAP, width), buffer_row, axis=0).astype(jnp.float32)
    normed, scale = norm_rows(x, user_gain)
    normed = normed.astype(jnp.bfloat16)
    whole = lax.all_gather(value_weight, "fsdp", axis=0, tiled=True)
    values = jnp.dot(normed, whole, preferred_element_type=jnp.float32)
    upstream = lax.dot_general(
        value_grad, whole, (((1,), (1,)), ((), ())), preferred_element_type=jnp.float32
    )
    values = values.astype(jnp.bfloat16)
    dx = norm_back(x, user_gain, scale, upstream)
    one_hot = (
        buffer_row[:, None] == lax.broadcasted_iota(jnp.int32, (hist_rows, groups * CAP), 1)
    ).astype(jnp.float32)
    summed = lax.dot_general(
        one_hot,
        dx,
        (((0,), (0,)), ((), ())),
        precision=lax.Precision.HIGHEST,
        preferred_element_type=jnp.float32,
    )
    returned = lax.all_to_all(
        summed.astype(jnp.bfloat16).reshape(groups, CAP, width),
        "dp",
        split_axis=0,
        concat_axis=0,
        tiled=True,
    )
    emb_grad = jnp.einsum("dcr,dck->rk", select, returned, preferred_element_type=jnp.float32)
    item_grad = norm_back(hidden, item_gain, item_scale, emb_grad)
    return (values, item_grad)


CHUNKS = 2
W_COPIES = 2


def iota(shape, dim):
    return lax.broadcasted_iota(jnp.int32, shape, dim)


def dot(a, b, ca=1, cb=0):
    return lax.dot_general(a, b, (((ca,), (cb,)), ((), ())), preferred_element_type=f32)


def fold(rows):
    half = rows.shape[1] // 2
    return jnp.concatenate([rows[:, :half], rows[:, half:]], axis=0)


def unfold(rows):
    return jnp.concatenate([rows[:CAP], rows[CAP:]], axis=1)


def stored_rows(hist, parts, item_rows):
    pool = parts.shape[1]
    named = (iota((pool, hist.shape[1]), 0) == hist).astype(f32).astype(bf16)
    found = dot(parts, named)
    return found[0:1] * item_rows + found[1:2]


def slots(wants, item_rows):
    lane = iota((item_rows, 128), 1)
    wanted = jnp.zeros((item_rows, 128), f32)
    for group, want in enumerate(wants):
        wanted = jnp.where(lane // CAP == group, want, wanted)
    before = (iota((item_rows, item_rows), 1) < iota((item_rows, item_rows), 0)).astype(f32)
    slot = dot(before.astype(bf16), wanted.astype(bf16))
    return jnp.where(slot == (lane % CAP).astype(f32), wanted, 0.0)


def kernel(
    groups, chips,
    item_gain_hbm, history_hbm, owner_hbm, user_gain_hbm, item_hidden, weight, value_grad,
    back_in, total_out, place_out, select_out,
    item_gain, history, owner, user_gain,
    hidden_buf, grad_buf, w_buf, hist_buf, emb_out, emb_in, sum_buf, x_out, x_in,
    part_own, part_out, part_in, up_out, up_in, back_out, total_buf, place_buf, select_buf,
    local_sem, out_sem, w_sem, hello, hist_send, hist_recv, emb_send, emb_recv, sum_send, sum_recv,
    x_send, x_recv, part_send, part_recv, up_send, up_recv, back_send, back_recv,
):
    here = lax.axis_index("dp")
    fsdp = lax.axis_index("fsdp")
    chip = fsdp // 2
    core = fsdp % 2
    item_rows, width = item_hidden.shape
    hist_rows = history.shape[1]
    rows = groups * CAP
    piece = width // chips
    cols = value_grad.shape[1] // CHUNKS
    peers = [lax.rem(here + k, groups) for k in range(1, groups)]
    mates = [lax.rem(chip + k, chips) for k in range(1, chips)]

    def dp_id(peer):
        return (peer, fsdp)

    def chip_id(mate):
        return (here, mate * 2 + core)

    sibling = (here, chip * 2 + 1 - core)

    barrier = pltpu.get_barrier_semaphore()
    group = [dp_id(p) for p in peers] + [chip_id(m) for m in mates]
    for target in group:
        pl.semaphore_signal(barrier, inc=1, device_id=target, device_id_type=MESH)

    loads = [
        pltpu.make_async_copy(src, dst, local_sem.at[k])
        for k, (src, dst) in enumerate([
            (history_hbm, history), (owner_hbm, owner), (value_grad, grad_buf),
            (item_hidden, hidden_buf), (item_gain_hbm, item_gain),
            (user_gain_hbm, user_gain), (weight, w_buf.at[core]),
        ])
    ]
    for load in loads:
        load.start()

    @pl.when(core == 0)
    def _():
        pl.semaphore_wait(barrier, len(group))
        pl.semaphore_signal(barrier, inc=1, device_id=sibling, device_id_type=MESH)

    @pl.when(core == 1)
    def _():
        pl.semaphore_wait(barrier, len(group) + 1)
        pl.semaphore_signal(hello, inc=1, device_id=sibling, device_id_type=MESH)

    stripe = weight.shape[0] // W_COPIES
    w_copies = [
        pltpu.make_async_remote_copy(
            src_ref=weight.at[pl.ds(k * stripe, stripe)],
            dst_ref=w_buf.at[core, pl.ds(k * stripe, stripe)],
            send_sem=w_sem.at[0, k], recv_sem=w_sem.at[1, k],
            device_id=sibling, device_id_type=MESH,
        )
        for k in range(W_COPIES)
    ]

    @pl.when(core == 1)
    def _():
        for copy in w_copies:
            copy.start()

    def remote(src, dst, send, recv, target):
        return pltpu.make_async_remote_copy(
            src_ref=src, dst_ref=dst, send_sem=send, recv_sem=recv,
            device_id=target, device_id_type=MESH,
        )

    sends = []

    def send_dp(out_of, into, send, recv):
        for k, peer in enumerate(peers):
            copy = remote(out_of(peer), into.at[here], send.at[k], recv.at[here], dp_id(peer))
            copy.start()
            sends.append(copy)

    def wait_dp(into, send, recv):
        for k, peer in enumerate(peers):
            remote(into.at[peer], into.at[peer], send.at[k], recv.at[peer], dp_id(peer)).wait_recv()

    def send_chip(out_of, into, send, recv):
        for k, mate in enumerate(mates):
            copy = remote(out_of(mate), into.at[chip], send.at[k], recv.at[chip], chip_id(mate))
            copy.start()
            sends.append(copy)

    def wait_chip(into, send, recv):
        for k, mate in enumerate(mates):
            remote(into.at[mate], into.at[mate], send.at[k], recv.at[mate], chip_id(mate)).wait_recv()

    send_dp(lambda peer: history_hbm, hist_buf, hist_send, hist_recv)
    loads[0].wait()
    hist_buf[here] = history[...]

    loads[1].wait()
    owner_row = owner[...]
    pool = owner_row.shape[1]
    div = (owner_row // item_rows).astype(f32)
    mod = (owner_row % item_rows).astype(f32)
    parts = jnp.where(iota((8, pool), 0) == 0, div, mod).astype(bf16)

    own = stored_rows(history[...], parts, item_rows)
    match = (iota((pool, hist_rows), 0).astype(f32) == own).astype(f32)
    wants = [
        jnp.max(match[e * item_rows : (e + 1) * item_rows], axis=1, keepdims=True)
        for e in range(groups)
    ]
    one_hot = slots(wants, item_rows)
    lane = iota((item_rows, 128), 1)
    stacked = jnp.concatenate(
        [jnp.where(lane // CAP == e, one_hot, 0.0) for e in range(groups)], axis=0
    )
    place = dot(stacked.astype(bf16), match.astype(bf16), 0, 0)[:rows]
    place = place.astype(bf16)
    place_buf[...] = place
    outs = [pltpu.make_async_copy(place_buf, place_out, out_sem.at[0])]
    outs[0].start()

    loads[2].wait()
    for c in range(CHUNKS):
        sum_buf[c, chip] = dot(place, grad_buf[:, c * cols : (c + 1) * cols]).astype(bf16)
        send_chip(
            lambda mate: sum_buf.at[c, chip], sum_buf.at[c], sum_send.at[c], sum_recv.at[c]
        )

    loads[3].wait()
    loads[4].wait()
    hidden = hidden_buf[...].astype(f32)
    item_scale = lax.rsqrt(jnp.mean(hidden * hidden, axis=1, keepdims=True) + 1e-6)
    item_emb = (hidden * item_scale * item_gain[...]).astype(bf16)

    wait_dp(hist_buf, hist_send, hist_recv)
    base = (here * item_rows).astype(f32)
    local_rows = iota((item_rows, hist_rows), 0).astype(f32) + base
    wants = []
    for t in range(groups):
        stored = stored_rows(hist_buf[t], parts, item_rows)
        wants.append(jnp.max((local_rows == stored).astype(f32), axis=1, keepdims=True))
    select = slots(wants, item_rows)[:, :rows].astype(bf16)
    select_buf[...] = select
    outs.append(pltpu.make_async_copy(select_buf, select_out, out_sem.at[1]))
    outs[1].start()
    outgoing = dot(select, item_emb, 0, 0)
    for t in range(groups):
        emb_out[t] = fold(outgoing[t * CAP : (t + 1) * CAP]).astype(bf16)
    send_dp(lambda peer: emb_out.at[peer], emb_in, emb_send, emb_recv)
    emb_in[here] = emb_out[here]

    @pl.when(core == 0)
    def _():
        pl.semaphore_wait(hello, 1)
        for copy in w_copies:
            copy.start()


    loads[5].wait()
    wait_dp(emb_in, emb_send, emb_recv)

    x = jnp.concatenate([unfold(emb_in[e].astype(f32)) for e in range(groups)], axis=0)
    scale = lax.rsqrt(jnp.mean(x * x, axis=1, keepdims=True) + 1e-6)
    normed = (x * scale * user_gain[...]).astype(bf16)
    for p in range(chips):
        x_out[p] = normed[:, p * piece : (p + 1) * piece]
    send_chip(lambda mate: x_out.at[mate], x_in, x_send, x_recv)
    x_in[chip] = x_out[chip]

    depth = weight.shape[0]

    def half_columns(half):
        return pl.ds(pl.multiple_of(half * depth, depth), depth)

    def up_half(half):
        up = jnp.zeros((chips * rows, depth), f32)
        for c in range(CHUNKS):
            sums = sum_buf[c].reshape(chips * rows, cols)
            up = up + dot(sums, w_buf[half, :, c * cols : (c + 1) * cols], 1, 1)
        up_out[:, :, half_columns(half)] = up.reshape(chips, rows, depth)

    def part_half(half, c):
        x_half = x_in[:, :, half_columns(half)].reshape(chips * rows, depth)
        part = dot(x_half, w_buf[half, :, c * cols : (c + 1) * cols])
        return part.reshape(chips, rows, cols)

    loads[6].wait()
    for c in range(CHUNKS):
        wait_chip(sum_buf.at[c], sum_send.at[c], sum_recv.at[c])
    up_half(core)
    wait_chip(x_in, x_send, x_recv)
    for c in range(CHUNKS):
        part_own[c] = part_half(core, c)

    for copy in w_copies:
        copy.wait()
    up_half(1 - core)
    send_chip(lambda mate: up_out.at[mate], up_in, up_send, up_recv)
    up_in[chip] = up_out[chip]
    for c in range(CHUNKS):
        part = part_own[c] + part_half(1 - core, c)
        part_own[c] = part
        part_out[c] = part.astype(bf16)
        send_chip(
            lambda mate: part_out.at[c, mate], part_in.at[c], part_send.at[c], part_recv.at[c]
        )

    wait_chip(up_in, up_send, up_recv)
    upstream = jnp.concatenate([up_in[p] for p in range(chips)], axis=1)
    unit = x * scale
    scaled = upstream * user_gain[...]
    block_sum = scale * (scaled - unit * jnp.mean(scaled * unit, axis=1, keepdims=True))
    for t in range(groups):
        back_out[t] = fold(block_sum[t * CAP : (t + 1) * CAP]).astype(bf16)
    send_dp(lambda peer: back_out.at[peer], back_in, back_send, back_recv)
    outs.append(pltpu.make_async_copy(back_out.at[here], back_in.at[here], out_sem.at[2]))
    outs[2].start()

    for c in range(CHUNKS):
        wait_chip(part_in.at[c], part_send.at[c], part_recv.at[c])
        total = part_own[c, chip]
        for mate in mates:
            total = total + part_in[c, mate].astype(f32)
        total_buf[c] = total.astype(bf16)
        out = pltpu.make_async_copy(total_buf.at[c], total_out.at[c], out_sem.at[3 + c])
        out.start()
        outs.append(out)

    wait_dp(back_in, back_send, back_recv)
    for out in outs:
        out.wait()
    for copy in sends:
        copy.wait_send()


def finish(
    groups, back_hbm, total_hbm, place_hbm, select_hbm, hidden_hbm, gain_hbm,
    values_out, item_grad_out,
    back, total, place, select, hidden_buf, gain, values, item_grad, load_sem, out_sem,
):
    loads = [
        pltpu.make_async_copy(src, dst, load_sem.at[k])
        for k, (src, dst) in enumerate([
            (hidden_hbm, hidden_buf), (gain_hbm, gain), (select_hbm, select), (back_hbm, back),
            (place_hbm, place), (total_hbm, total),
        ])
    ]
    for load in loads:
        load.start()
    loads[0].wait()
    loads[1].wait()
    hidden = hidden_buf[...].astype(f32)
    scale = lax.rsqrt(jnp.mean(hidden * hidden, axis=1, keepdims=True) + 1e-6)
    loads[2].wait()
    loads[3].wait()
    returned = jnp.concatenate([unfold(back[t].astype(f32)) for t in range(groups)], axis=0)
    emb_grad = dot(select[...], returned.astype(bf16))
    unit = hidden * scale
    scaled = emb_grad * gain[...]
    item_grad[...] = scale * (scaled - unit * jnp.mean(scaled * unit, axis=1, keepdims=True))
    grad_copy = pltpu.make_async_copy(item_grad, item_grad_out, out_sem.at[0])
    grad_copy.start()
    loads[4].wait()
    loads[5].wait()
    named = place[...]
    cols = total.shape[2]
    for c in range(CHUNKS):
        values[:, c * cols : (c + 1) * cols] = dot(named, total[c], 0, 0).astype(bf16)
    values_copy = pltpu.make_async_copy(values, values_out, out_sem.at[1])
    values_copy.start()
    grad_copy.wait()
    values_copy.wait()


def local_moving_rows(
    item_hidden, item_gain, history, owner_map, user_gain, value_weight, value_grad
):
    groups = lax.axis_size("dp")
    chips = lax.axis_size("fsdp") // 2
    item_rows, width = item_hidden.shape
    hist_rows, out_width = value_grad.shape
    rows = groups * CAP
    depth = value_weight.shape[0]
    piece = 2 * depth
    cols = out_width // CHUNKS
    hbm = pl.BlockSpec(memory_space=pl.ANY)

    def dma(*counts):
        return pltpu.SemaphoreType.DMA(counts)

    folded = (groups, 2 * CAP, width // 2)
    back, total, place, select = pl.pallas_call(
        functools.partial(kernel, groups, chips),
        out_shape=(
            jax.ShapeDtypeStruct(folded, bf16),
            jax.ShapeDtypeStruct((CHUNKS, rows, cols), bf16),
            jax.ShapeDtypeStruct((rows, hist_rows), bf16),
            jax.ShapeDtypeStruct((item_rows, rows), bf16),
        ),
        in_specs=[hbm] * 7,
        out_specs=(hbm,) * 4,
        scratch_shapes=[
            pltpu.VMEM((1, width), f32),
            pltpu.VMEM((1, hist_rows), jnp.int32),
            pltpu.VMEM((1, owner_map.shape[1]), jnp.int32),
            pltpu.VMEM((1, width), f32),
            pltpu.VMEM((item_rows, width), bf16),
            pltpu.VMEM((hist_rows, out_width), bf16),
            pltpu.VMEM((2, depth, out_width), bf16),
            pltpu.VMEM((groups, 1, hist_rows), jnp.int32),
            pltpu.VMEM(folded, bf16),
            pltpu.VMEM(folded, bf16),
            pltpu.VMEM((CHUNKS, chips, rows, cols), bf16),
            pltpu.VMEM((chips, rows, piece), bf16),
            pltpu.VMEM((chips, rows, piece), bf16),
            pltpu.VMEM((CHUNKS, chips, rows, cols), f32),
            pltpu.VMEM((CHUNKS, chips, rows, cols), bf16),
            pltpu.VMEM((CHUNKS, chips, rows, cols), bf16),
            pltpu.VMEM((chips, rows, piece), f32),
            pltpu.VMEM((chips, rows, piece), f32),
            pltpu.VMEM(folded, bf16),
            pltpu.VMEM((CHUNKS, rows, cols), bf16),
            pltpu.VMEM((rows, hist_rows), bf16),
            pltpu.VMEM((item_rows, rows), bf16),
            dma(7), dma(3 + CHUNKS), dma(2, W_COPIES), pltpu.SemaphoreType.REGULAR,
            dma(groups), dma(groups), dma(groups), dma(groups),
            dma(CHUNKS, chips), dma(CHUNKS, chips), dma(chips), dma(chips),
            dma(CHUNKS, chips), dma(CHUNKS, chips), dma(chips), dma(chips),
            dma(groups), dma(groups),
        ],
        compiler_params=pltpu.CompilerParams(
            collective_id=0, has_side_effects=True, vmem_limit_bytes=60 * 2**20
        ),
    )(
        item_gain[None, :], history[None, :], owner_map, user_gain[None, :],
        item_hidden, value_weight, value_grad,
    )
    return pl.pallas_call(
        functools.partial(finish, groups),
        out_shape=(
            jax.ShapeDtypeStruct((hist_rows, out_width), bf16),
            jax.ShapeDtypeStruct((item_rows, width), f32),
        ),
        in_specs=[hbm] * 6,
        out_specs=(hbm,) * 2,
        scratch_shapes=[
            pltpu.VMEM(folded, bf16),
            pltpu.VMEM((CHUNKS, rows, cols), bf16),
            pltpu.VMEM((rows, hist_rows), bf16),
            pltpu.VMEM((item_rows, rows), bf16),
            pltpu.VMEM((item_rows, width), bf16),
            pltpu.VMEM((1, width), f32),
            pltpu.VMEM((hist_rows, out_width), bf16),
            pltpu.VMEM((item_rows, width), f32),
            dma(6), dma(2),
        ],
        compiler_params=pltpu.CompilerParams(vmem_limit_bytes=60 * 2**20),
    )(back, total, place, select, item_hidden, item_gain[None, :])


def local(item_hidden, item_gain, history, owner_map, user_gain, value_weight, value_grad):
    chips = lax.axis_size("fsdp") // 2
    moved = 2 * chips * lax.axis_size("dp") * CAP
    by_rows = moved <= value_grad.shape[1] and lax.axis_size("dp") * CAP <= 128
    plan = local_moving_rows if by_rows else local_moving_weight
    return plan(
        item_hidden, item_gain, history, owner_map, user_gain, value_weight, value_grad
    )


def solution(mesh):
    in_specs = (
        P(("dp", "fsdp"), None),
        P(),
        P(("dp", "fsdp")),
        P("fsdp", None),
        P(),
        P("fsdp", None),
        P(("dp", "fsdp"), None),
    )
    out_specs = (P(("dp", "fsdp"), None), P(("dp", "fsdp"), None))
    return jax.shard_map(local, mesh=mesh, in_specs=in_specs, out_specs=out_specs, check_vma=False)
```
